32 devices in a mesh: gz: 4 (over y, x), gx: 8 (over z, core).
Axes of the slice: x: 2, y: 2, z: 4, core: 2. Of those that a mesh axis runs over, the one named last changes fastest.
Arguments:
- adj_fields: float32 [6, 128, 128, 8, 128], P(None, 'gx', 'gz'), may hold values from -6 to 6
- coef_e: float32 [128, 128, 8, 128], P('gx', 'gz'), may hold values from 0.1 to 0.6
- plane_z: int32 [2], replicated, may hold values from 0 to 127
- snap_index: int32 [1], replicated, may hold values from 0 to 2
- fwd_snaps: float32 [4, 2, 3, 128, 1024], P(None, None, None, 'gx', 'gz'), may hold values from -6 to 6
- design: float32 [2, 128, 1024], P(None, 'gx', 'gz'), may hold values from 0 to 1
- sens_in: float32 [2, 128, 1024], P(None, 'gx', 'gz'), may hold values from -6 to 6
Outputs:
- new_fields: float32 [6, 128, 128, 8, 128], P(None, 'gx', 'gz')
- gradient: float32 [2, 128, 1024], P(None, 'gx', 'gz')
The draws below stay inside these ranges and needn't reach their ends.
Inputs may be any that keep to these rules, and one draw needn't show every extreme that they name: `plane_z`: the two design planes may lie in the same or in different z slabs.
All inputs are finite; a program needn't handle non-finite values.
Results may differ from the reference program's by a relative error of at most 0.00016.
Values sent between devices are 32-bit elements; how exact they have to be, the bound alone decides.
A program may use at most 128 MiB of HBM per device.

```python
import math
import jax
import jax.numpy as jnp
from jax import lax

NY = 1024
R = 8
STEPS = 2
SNAP = 4
NX = 128
NZ = 128


def shard_levels(stream_key, extent, cuts, least, top_value):
    level = 1.0
    for dim, shards_of in cuts:
        draws = jax.random.uniform(jax.random.fold_in(jax.random.fold_in(stream_key, 6), dim), (shards_of,), jnp.float32, least / len(cuts), top_value / len(cuts))
        level = level * jnp.repeat(jnp.exp(draws), extent[dim] // shards_of).reshape((-1,) + (1,) * (len(extent) - 1 - dim))
    return level


def gaussian(stream_key, dims, scale, limit, split=(), kind=jnp.bfloat16):
    drawn = scale * jax.random.normal(stream_key, dims, jnp.float32)
    if split:
        drawn = drawn * shard_levels(stream_key, dims, split, -0.22, 0.18)
    return jnp.clip(drawn, -limit, limit).astype(kind)


def setup_inputs(seed: int = 0) -> dict:
    streams_of = jax.random.split(jax.random.key(seed), 8)
    adj_fields = gaussian(streams_of[0], (6, NX, NZ, NY // 128, 128), 1.0, 6.0, ((1, 8), (2, 4)), jnp.float32)
    coef_e = jnp.clip(jnp.exp(math.log(0.6) - 1.7917595 * jax.random.uniform(streams_of[1], (NX, NZ, NY // 128, 128), jnp.float32) ** shard_levels(streams_of[1], (NX, NZ, NY // 128, 128), ((0, 8), (1, 4)), -0.2, 0.2)), 0.1, 0.6)
    plane_z = jax.random.randint(streams_of[2], (2,), 0, NZ).astype(jnp.int32)
    snap_index = jax.random.randint(streams_of[3], (1,), 0, SNAP - STEPS + 1).astype(jnp.int32)
    fwd_snaps = gaussian(streams_of[4], (SNAP, 2, 3, NX, NY), 1.0, 6.0, ((3, 8), (4, 4)), jnp.float32)
    design = jnp.clip(1.0 * jax.random.uniform(streams_of[5], (2, NX, NY), jnp.float32) ** shard_levels(streams_of[5], (2, NX, NY), ((1, 8), (2, 4)), -0.2, 0.2), 0.0, 1.0)
    sens_in = gaussian(streams_of[6], (2, NX, NY), 1.0, 6.0, ((1, 8), (2, 4)), jnp.float32)
    return dict(adj_fields=adj_fields, coef_e=coef_e, plane_z=plane_z, snap_index=snap_index, fwd_snaps=fwd_snaps, design=design, sens_in=sens_in)


magnetic_step = 0.5
sharpness = 8.0
threshold = 0.5

def cone_table(radius):
    raw = [[max(0.0, radius - math.sqrt((first - radius) ** 2 + (second - radius) ** 2)) for second in range(2 * radius + 1)] for first in range(2 * radius + 1)]
    total = sum((sum(line) for line in raw))
    return [[entry / total for entry in line] for line in raw]

def forward(component, direction):
    widths = [(0, 1) if number == direction else (0, 0) for number in range(3)]
    padded = jnp.pad(component, widths)
    return lax.slice_in_dim(padded, 1, None, axis=direction) - component

def backward(component, direction):
    widths = [(1, 0) if number == direction else (0, 0) for number in range(3)]
    padded = jnp.pad(component, widths)
    return component - lax.slice_in_dim(padded, 0, component.shape[direction], axis=direction)

def cone_filter(values):
    weights_table = cone_table(R)
    padded = jnp.pad(values, ((0, 0), (R, R), (R, R)))
    row_count, col_count = (values.shape[1], values.shape[2])
    filtered_sum = jnp.zeros(values.shape, jnp.float32)
    for offset_x in range(2 * R + 1):
        for offset_y in range(2 * R + 1):
            weight = weights_table[offset_x][offset_y]
            filtered_sum = filtered_sum + weight * padded[:, offset_x:offset_x + row_count, offset_y:offset_y + col_count]
    return filtered_sum

def projection_slope(filtered):
    scale_down = math.tanh(sharpness * threshold) + math.tanh(sharpness * (1.0 - threshold))
    return sharpness * (1.0 - jnp.tanh(sharpness * (filtered - threshold)) ** 2) / scale_down

def reference(adj_fields, coef_e, plane_z, snap_index, fwd_snaps, design, sens_in):
    flat_fields = adj_fields.reshape(6, NX, NZ, NY)
    flat_coef = coef_e.reshape(NX, NZ, NY)
    electric = flat_fields[0:3]
    magnetic = flat_fields[3:6]
    sensitivity = sens_in
    for step in range(STEPS):
        electric_x, electric_y, electric_z = (electric[0], electric[1], electric[2])
        rotation = jnp.stack([forward(electric_z, 2) - forward(electric_y, 1), forward(electric_x, 1) - forward(electric_z, 0), forward(electric_y, 0) - forward(electric_x, 2)])
        magnetic = magnetic + magnetic_step * rotation
        magnetic_x, magnetic_y, magnetic_z = (magnetic[0], magnetic[1], magnetic[2])
        rotation_back = jnp.stack([backward(magnetic_z, 2) - backward(magnetic_y, 1), backward(magnetic_x, 1) - backward(magnetic_z, 0), backward(magnetic_y, 0) - backward(magnetic_x, 2)])
        electric = electric - flat_coef[None] * rotation_back
        snapshot = lax.dynamic_index_in_dim(fwd_snaps, (snap_index[0] + step).astype(jnp.int32), 0, keepdims=False)
        layers = jnp.stack([lax.dynamic_index_in_dim(electric, plane_z[plane_index].astype(jnp.int32), 2, keepdims=False) for plane_index in range(2)])
        sensitivity = sensitivity + lax.optimization_barrier(jnp.sum(snapshot * layers, axis=1))
    filtered = cone_filter(design)
    gradient = cone_filter(sensitivity * projection_slope(filtered))
    new_fields = jnp.concatenate([electric, magnetic], axis=0).reshape(6, NX, NZ, NY // 128, 128)
    return (new_fields, gradient)
```

```python
import functools
import math

import jax
import jax.numpy as jnp
from jax import lax
from jax.experimental import pallas as pl
from jax.experimental.pallas import tpu as pltpu
from jax.sharding import PartitionSpec as P

R = 8
STEPS = 2
PLANES = 2
COMPS = 3
IMAGES = STEPS * PLANES * COMPS + 2 * PLANES
DESIGN = STEPS * PLANES * COMPS
SENS = DESIGN + PLANES
LANES = 128
SUBS = 8

magnetic_step = 0.5
sharpness = 8.0
threshold = 0.5

MESH = pl.DeviceIdType.MESH


def cone_table(radius):
    raw = [
        [max(0.0, radius - math.sqrt(a * a + b * b)) for b in range(radius + 1)]
        for a in range(radius + 1)
    ]
    total = sum(
        raw[abs(a)][abs(b)]
        for a in range(-radius, radius + 1)
        for b in range(-radius, radius + 1)
    )
    return [[entry / total for entry in line] for line in raw]


def projection_slope(filtered):
    scale_down = math.tanh(sharpness * threshold) + math.tanh(sharpness * (1.0 - threshold))
    return sharpness * (1.0 - jnp.tanh(sharpness * (filtered - threshold)) ** 2) / scale_down


def iota(shape, dim):
    return lax.broadcasted_iota(jnp.int32, shape, dim)


def ahead_y(v):
    n = v.ndim
    turned = pltpu.roll(v, LANES - 1, n - 1)
    carried = pltpu.roll(turned, SUBS - 1, n - 2)
    carried = jnp.where(iota(v.shape, n - 2) == SUBS - 1, 0.0, carried)
    return jnp.where(iota(v.shape, n - 1) == LANES - 1, carried, turned)


def behind_y(v):
    n = v.ndim
    turned = pltpu.roll(v, 1, n - 1)
    carried = pltpu.roll(turned, 1, n - 2)
    carried = jnp.where(iota(v.shape, n - 2) == 0, 0.0, carried)
    return jnp.where(iota(v.shape, n - 1) == 0, carried, turned)


def cone(ref, rows):
    table = cone_table(R)
    sums = [ref[:, :, R : R + rows]]
    for a in range(1, R):
        sums.append(ref[:, :, R - a : R - a + rows] + ref[:, :, R + a : R + a + rows])
    blocks = ref.shape[0]
    out = None
    for b in range(R):
        total = None
        for a in range(R):
            if table[a][b] > 0.0:
                term = table[a][b] * sums[a]
                total = term if total is None else total + term
        mid = total[1 : blocks - 1]
        if b == 0:
            out = mid
            continue
        lane = iota(mid.shape, 3)
        upper = jnp.where(lane < b, total[2:], mid)
        lower = jnp.where(lane >= LANES - b, total[: blocks - 2], mid)
        out = out + pltpu.roll(upper, LANES - b, 3) + pltpu.roll(lower, b, 3)
    return out


def kernel(
    gxn,
    gzn,
    fields,
    coef,
    plane_z,
    snap_index,
    fwd,
    design,
    sens_in,
    out,
    gradient,
    E,
    H,
    C,
    exr,
    ezr,
    gxr,
    gzr,
    cxr,
    czr,
    gxs,
    gzs,
    AG,
    DF,
    L,
    PT,
    RC,
    WV,
    step_send,
    step_recv,
    ag_send,
    ag_recv,
    rc_send,
    rc_recv,
    row_send,
    row_recv,
    load_sem,
    store_sem,
):
    X, Z = coef.shape[0], coef.shape[1]
    NB = coef.shape[2]
    TB = NB // gzn
    WB = TB + 2
    gx, gz = lax.axis_index("gx"), lax.axis_index("gz")
    has_xm, has_xp = gx > 0, gx < gxn - 1
    has_zm, has_zp = gz > 0, gz < gzn - 1

    def load(index, src, dst):
        return pltpu.make_async_copy(src, dst, load_sem.at[index])

    half = X // 2
    loads = [
        load(0, fields.at[0:3, X - 1], E.at[:, X - 1, 0:Z]),
        load(1, fields.at[3:6, X - 1], H.at[:, X, 1 : Z + 1]),
        load(2, fields.at[0:3, 0 : X - 1, Z - 1], E.at[:, 0 : X - 1, Z - 1]),
        load(3, fields.at[3:6, 0 : X - 1, Z - 1], H.at[:, 1:X, Z]),
        load(4, fields.at[0:3, 0:half, 0 : Z - 1], E.at[:, 0:half, 0 : Z - 1]),
        load(5, fields.at[3:6, 0:half, 0 : Z - 1], H.at[:, 1 : half + 1, 1:Z]),
        load(6, fields.at[0:3, half : X - 1, 0 : Z - 1], E.at[:, half : X - 1, 0 : Z - 1]),
        load(7, fields.at[3:6, half : X - 1, 0 : Z - 1], H.at[:, half + 1 : X, 1:Z]),
        load(8, coef, C),
    ]
    for copy in loads:
        copy.start()

    barrier = pltpu.get_barrier_semaphore()

    def greet(x, z):
        pl.semaphore_signal(barrier, inc=1, device_id={"gx": x, "gz": z}, device_id_type=MESH)

    for condition, x, z in (
        (has_xm, gx - 1, gz),
        (has_xp, gx + 1, gz),
        (has_xp & has_zm, gx + 1, gz - 1),
        (has_xm & has_zp, gx - 1, gz + 1),
    ):
        pl.when(condition)(functools.partial(greet, x, z))
    for d in range(1, gzn):
        greet(gx, lax.rem(gz + d, gzn))

    snap = snap_index[0]
    for block in range(TB):
        lanes = slice(block * LANES, (block + 1) * LANES)
        place = 2 + gz * TB + block
        for step in range(STEPS):
            for p in range(PLANES):
                for c in range(COMPS):
                    AG[place, (step * PLANES + p) * COMPS + c] = fwd[snap + step, p, c, :, lanes]
        AG[place, DESIGN:SENS] = design[:, :, lanes]
        AG[place, SENS:] = sens_in[:, :, lanes]
    pads = jnp.zeros((2, 2 * PLANES, X, LANES), jnp.float32)
    AG[0:2, DESIGN:] = pads
    AG[NB + 2 :, DESIGN:] = pads
    PT[0] = jnp.zeros(PT.shape[1:], jnp.float32)
    PT[NB + 1] = jnp.zeros(PT.shape[1:], jnp.float32)
    DF[:, :, 0:R] = jnp.zeros((TB + 4, PLANES, R, LANES), jnp.float32)
    DF[:, :, R + X :] = jnp.zeros((TB + 4, PLANES, R, LANES), jnp.float32)

    E[:, X] = jnp.zeros((COMPS, Z + 1, SUBS, LANES), jnp.float32)
    E[:, 0:X, Z] = jnp.zeros((COMPS, X, SUBS, LANES), jnp.float32)
    H[:, 0] = jnp.zeros((COMPS, Z + 1, SUBS, LANES), jnp.float32)
    H[:, 1:, 0] = jnp.zeros((COMPS, X, SUBS, LANES), jnp.float32)

    met = (
        has_xm.astype(jnp.int32)
        + has_xp.astype(jnp.int32)
        + (has_xp & has_zm).astype(jnp.int32)
        + (has_xm & has_zp).astype(jnp.int32)
        + (gzn - 1)
    )
    pl.semaphore_wait(barrier, met)

    def remote(src, dst, send, recv, x, z):
        return pltpu.make_async_remote_copy(
            src_ref=src,
            dst_ref=dst,
            send_sem=send,
            recv_sem=recv,
            device_id={"gx": x, "gz": z},
            device_id_type=MESH,
        )

    def step_copies(s):
        electric = fields if s == 0 else E

        def make(k, src, dst, x, z):
            return remote(src, dst, step_send.at[s, k], step_recv.at[s, k], x, z)

        return dict(
            ex=(make(0, electric.at[1:3, 0, 0:Z], exr.at[s], gx - 1, gz), has_xm, has_xp),
            ez=(make(1, electric.at[0:2, 0:X, 0], ezr.at[s], gx, gz - 1), has_zm, has_zp),
            cx=(
                make(2, electric.at[0, X - 1, 0], cxr.at[s], gx + 1, gz - 1),
                has_xp & has_zm,
                has_xm & has_zp,
            ),
            cz=(
                make(3, electric.at[2, 0, Z - 1], czr.at[s], gx - 1, gz + 1),
                has_xm & has_zp,
                has_xp & has_zm,
            ),
            gx=(make(4, gxs.at[s], gxr.at[s], gx + 1, gz), has_xp, has_xm),
            gz=(make(5, gzs.at[s], gzr.at[s], gx, gz + 1), has_zp, has_zm),
        )

    def start(item):
        pl.when(item[1])(item[0].start)

    def finish_send(item):
        pl.when(item[1])(item[0].wait_send)

    def fill_sends(s):
        E[0, X - 1, Z] = jnp.zeros((SUBS, LANES), jnp.float32)
        E[2, X, Z - 1] = jnp.zeros((SUBS, LANES), jnp.float32)
        ex, ey, ez = (E[c, X - 1, 0:Z] for c in range(3))
        gxs[s, 0] = H[1, X, 1:] + magnetic_step * (E[0, X - 1, 1 : Z + 1] - ex + ez)
        gxs[s, 1] = H[2, X, 1:] - magnetic_step * (ey + ahead_y(ex) - ex)
        ex, ey, ez = (E[c, 0:X, Z - 1] for c in range(3))
        gzs[s, 0] = H[0, 1:, Z] + magnetic_step * (ahead_y(ez) - ez + ey)
        gzs[s, 1] = H[1, 1:, Z] - magnetic_step * (ex + E[2, 1 : X + 1, Z - 1] - ez)

    def receive(s, copies):
        @pl.when(has_xp)
        def _():
            copies["ex"][0].wait_recv()
            E[1:3, X, 0:Z] = exr[s]

        @pl.when(has_zp)
        def _():
            copies["ez"][0].wait_recv()
            E[0:2, 0:X, Z] = ezr[s]

        @pl.when(has_xm)
        def _():
            copies["gx"][0].wait_recv()
            H[1, 0, 1:] = gxr[s, 0] - magnetic_step * E[2, 0, 0:Z]
            H[2, 0, 1:] = gxr[s, 1] + magnetic_step * E[1, 0, 0:Z]

        @pl.when(has_zm)
        def _():
            copies["gz"][0].wait_recv()
            H[0, 1:, 0] = gzr[s, 0] - magnetic_step * E[1, 0:X, 0]
            H[1, 1:, 0] = gzr[s, 1] + magnetic_step * E[0, 0:X, 0]

        @pl.when(has_xm & has_zp)
        def _():
            copies["cx"][0].wait_recv()
            H[1, 0, Z] = H[1, 0, Z] + magnetic_step * cxr[s]

        @pl.when(has_xp & has_zm)
        def _():
            copies["cz"][0].wait_recv()
            H[1, X, 0] = H[1, X, 0] - magnetic_step * czr[s]

    def update_h(x, z, n):
        here, next_z = pl.ds(z, n), pl.ds(z + 1, n)
        ex, ey, ez = (E[c, x, here] for c in range(3))
        ex_z, ey_z = E[0, x, next_z], E[1, x, next_z]
        ey_x, ez_x = E[1, x + 1, here], E[2, x + 1, here]
        H[0, x + 1, next_z] += magnetic_step * ((ahead_y(ez) - ez) - (ey_z - ey))
        H[1, x + 1, next_z] += magnetic_step * ((ex_z - ex) - (ez_x - ez))
        H[2, x + 1, next_z] += magnetic_step * ((ey_x - ey) - (ahead_y(ex) - ex))

    def new_e(x, z, n):
        before, here = pl.ds(z, n), pl.ds(z + 1, n)
        own = pl.ds(z, n)
        hx, hy, hz = (H[c, x + 1, here] for c in range(3))
        hx_z, hy_z = H[0, x + 1, before], H[1, x + 1, before]
        hy_x, hz_x = H[1, x, here], H[2, x, here]
        factor = C[x, own]
        return (
            E[0, x, own] - factor * ((hz - behind_y(hz)) - (hy - hy_z)),
            E[1, x, own] - factor * ((hx - hx_z) - (hz - hz_x)),
            E[2, x, own] - factor * ((hy - hy_x) - (hx - behind_y(hx))),
        )

    def chunks(stop, width=8):
        return [(z, min(width, stop - z)) for z in range(0, stop, width)]

    def sweep_h(x_stop, z_stop):
        @pl.loop(0, x_stop)
        def _(x):
            for z, n in chunks(z_stop):
                update_h(x, z, n)

    def sweep_e(x_start, x_stop):
        @pl.loop(x_start, x_stop)
        def _(x):
            for z, n in chunks(Z):
                E[0, x, z : z + n], E[1, x, z : z + n], E[2, x, z : z + n] = new_e(x, z, n)

    def layer_of(p):
        local = plane_z[p] - gz * Z
        inside = (local >= 0) & (local < Z)
        return jnp.clip(local, 0, Z - 1), jnp.where(inside, 1.0, 0.0).astype(jnp.float32)

    def products(step):
        @pl.loop(0, NB)
        def _(block):
            for p in range(PLANES):
                total = None
                for c in range(COMPS):
                    image = (step * PLANES + p) * COMPS + c
                    term = AG[block + 2, image] * L[step, p, c, :, block]
                    total = term if total is None else total + term
                if step:
                    total = PT[block + 1, p] + total
                PT[block + 1, p] = total

    copies = step_copies(0)
    for name in ("ex", "ez", "cx", "cz"):
        start(copies[name])
    for copy in loads[:4]:
        copy.wait()
    fill_sends(0)
    start(copies["gx"])
    start(copies["gz"])
    tile = pl.ds(2 + gz * TB, TB)
    gathers = [
        remote(AG.at[tile], AG.at[tile], ag_send.at[d], ag_recv.at[d], gx, lax.rem(gz + d, gzn))
        for d in range(1, gzn)
    ]
    for copy in gathers:
        copy.start()
    for copy in loads[4:]:
        copy.wait()
    receive(0, copies)
    sweep_h(X, Z)
    sweep_e(0, X)
    for item in copies.values():
        finish_send(item)

    copies = step_copies(1)
    for name in ("ex", "ez", "cx", "cz"):
        start(copies[name])
    fill_sends(1)
    start(copies["gx"])
    start(copies["gz"])
    sweep_h(X - 1, Z - 1)
    for p in range(PLANES):
        layer, inside = layer_of(p)
        for c in range(COMPS):
            L[0, p, c] = E[c, 0:X, layer] * inside
    for d in range(1, gzn):
        source = pl.ds(2 + lax.rem(gz + gzn - d, gzn) * TB, TB)
        remote(
            AG.at[tile], AG.at[source], ag_send.at[d], ag_recv.at[d], gx, lax.rem(gz + d, gzn)
        ).wait_recv()
    around = pl.ds(gz * TB, TB + 4)
    rows = [
        (
            remote(
                AG.at[around, DESIGN:SENS, X - R : X],
                DF.at[:, :, 0:R],
                row_send.at[0],
                row_recv.at[0],
                gx + 1,
                gz,
            ),
            has_xp,
            has_xm,
        ),
        (
            remote(
                AG.at[around, DESIGN:SENS, 0:R],
                DF.at[:, :, R + X : X + 2 * R],
                row_send.at[1],
                row_recv.at[1],
                gx - 1,
                gz,
            ),
            has_xm,
            has_xp,
        ),
    ]
    for item in rows:
        start(item)
    products(0)
    receive(1, copies)

    @pl.loop(0, X - 1)
    def _(x):
        update_h(x, Z - 1, 1)

    for z, n in chunks(Z):
        update_h(X - 1, z, n)
    for item in copies.values():
        finish_send(item)
    store_h = pltpu.make_async_copy(H.at[:, 1:, 1:], out.at[3:6], store_sem.at[0])
    store_h.start()

    for p in range(PLANES):
        layer, inside = layer_of(p)

        @pl.loop(0, X)
        def _(x):
            for c, value in enumerate(new_e(x, layer, 1)):
                L[1, p, c, x] = value[0] * inside

    products(1)
    partials = []
    for d in range(1, gzn):
        peer = lax.rem(gz + d, gzn)
        partials.append(
            remote(
                PT.at[pl.ds(peer * TB, WB)],
                RC.at[d],
                rc_send.at[d],
                rc_recv.at[d],
                gx,
                peer,
            )
        )
    for copy in partials:
        copy.start()
    sweep_e(0, half)
    store_low = pltpu.make_async_copy(
        E.at[:, 0:half, 0:Z], out.at[0:3, 0:half], store_sem.at[1]
    )
    store_low.start()
    sweep_e(half, X)
    store_high = pltpu.make_async_copy(
        E.at[:, half:X, 0:Z], out.at[0:3, half:X], store_sem.at[2]
    )
    store_high.start()

    DF[:, :, R : R + X] = AG[around, DESIGN:SENS]
    for item in rows:
        pl.when(item[2])(item[0].wait_recv)
    slope = projection_slope(cone(DF, X))
    total = AG[pl.ds(gz * TB + 1, WB), SENS:] + PT[pl.ds(gz * TB, WB)]
    for d, copy in enumerate(partials, 1):
        copy.wait_recv()
        total = total + RC[d]
    WV[:, :, R : R + X] = total * slope
    edges = [
        (
            remote(
                WV.at[:, :, X : X + R], WV.at[:, :, 0:R], row_send.at[2], row_recv.at[2], gx + 1, gz
            ),
            has_xp,
            has_xm,
        ),
        (
            remote(
                WV.at[:, :, R : 2 * R],
                WV.at[:, :, R + X : X + 2 * R],
                row_send.at[3],
                row_recv.at[3],
                gx - 1,
                gz,
            ),
            has_xm,
            has_xp,
        ),
    ]
    for item in edges:
        start(item)
    none = jnp.zeros((WB, PLANES, R, LANES), jnp.float32)

    @pl.when(gx == 0)
    def _():
        WV[:, :, 0:R] = none

    @pl.when(gx == gxn - 1)
    def _():
        WV[:, :, R + X :] = none

    for item in edges:
        pl.when(item[2])(item[0].wait_recv)
    result = cone(WV, X)
    for block in range(TB):
        gradient[:, :, block * LANES : (block + 1) * LANES] = result[block]

    for copy in gathers + partials:
        copy.wait_send()
    for item in rows + edges:
        finish_send(item)
    for copy in (store_h, store_low, store_high):
        copy.wait()


def shards(adj_fields, coef_e, plane_z, snap_index, fwd_snaps, design, sens_in):
    gxn, gzn = lax.axis_size("gx"), lax.axis_size("gz")
    X, Z, NB = coef_e.shape[0], coef_e.shape[1], coef_e.shape[2]
    TB = NB // gzn
    WB = TB + 2
    cell = (SUBS, LANES)

    def vmem(*shape):
        return pltpu.VMEM(shape, jnp.float32)

    hbm = pl.BlockSpec(memory_space=pl.ANY)
    smem = pl.BlockSpec(memory_space=pltpu.SMEM)
    local = pl.BlockSpec(memory_space=pltpu.VMEM)
    dma = pltpu.SemaphoreType.DMA
    return pl.pallas_call(
        functools.partial(kernel, gxn, gzn),
        out_shape=(
            jax.ShapeDtypeStruct(adj_fields.shape, jnp.float32),
            jax.ShapeDtypeStruct(design.shape, jnp.float32),
        ),
        in_specs=[hbm, hbm, smem, smem, local, local, local],
        out_specs=(hbm, local),
        scratch_shapes=[
            vmem(COMPS, X + 1, Z + 1, *cell),
            vmem(COMPS, X + 1, Z + 1, *cell),
            vmem(X, Z, *cell),
            vmem(STEPS, 2, Z, *cell),
            vmem(STEPS, 2, X, *cell),
            vmem(STEPS, 2, Z, *cell),
            vmem(STEPS, 2, X, *cell),
            vmem(STEPS, *cell),
            vmem(STEPS, *cell),
            vmem(STEPS, 2, Z, *cell),
            vmem(STEPS, 2, X, *cell),
            vmem(NB + 4, IMAGES, X, LANES),
            vmem(TB + 4, PLANES, X + 2 * R, LANES),
            vmem(STEPS, PLANES, COMPS, X, *cell),
            vmem(NB + 2, PLANES, X, LANES),
            vmem(gzn, WB, PLANES, X, LANES),
            vmem(WB, PLANES, X + 2 * R, LANES),
            dma((STEPS, 6)),
            dma((STEPS, 6)),
            dma((gzn,)),
            dma((gzn,)),
            dma((gzn,)),
            dma((gzn,)),
            dma((4,)),
            dma((4,)),
            dma((9,)),
            dma((3,)),
        ],
        compiler_params=pltpu.CompilerParams(
            collective_id=0, has_side_effects=True, vmem_limit_bytes=40 * 2**20
        ),
    )(adj_fields, coef_e, plane_z, snap_index, fwd_snaps, design, sens_in)


def solution(mesh):
    in_specs = (
        P(None, "gx", "gz", None, None),
        P("gx", "gz", None, None),
        P(),
        P(),
        P(None, None, None, "gx", "gz"),
        P(None, "gx", "gz"),
        P(None, "gx", "gz"),
    )
    out_specs = (P(None, "gx", "gz", None, None), P(None, "gx", "gz"))
    return jax.shard_map(shards, mesh=mesh, in_specs=in_specs, out_specs=out_specs, check_vma=False)
```

```python
import functools
import math

import jax
import jax.numpy as jnp
from jax import lax
from jax.experimental import pallas as pl
from jax.experimental.pallas import tpu as pltpu
from jax.sharding import PartitionSpec as P

R = 8
STEPS = 2
PLANES = 2
COMPS = 3
IMAGES = STEPS * PLANES * COMPS + 2 * PLANES
DESIGN = STEPS * PLANES * COMPS
SENS = DESIGN + PLANES
LANES = 128
SUBS = 8

magnetic_step = 0.5
sharpness = 8.0
threshold = 0.5

MESH = pl.DeviceIdType.MESH


def cone_table(radius):
    raw = [
        [max(0.0, radius - math.sqrt(a * a + b * b)) for b in range(radius + 1)]
        for a in range(radius + 1)
    ]
    total = sum(
        raw[abs(a)][abs(b)]
        for a in range(-radius, radius + 1)
        for b in range(-radius, radius + 1)
    )
    return [[entry / total for entry in line] for line in raw]


def projection_slope(filtered):
    scale_down = math.tanh(sharpness * threshold) + math.tanh(sharpness * (1.0 - threshold))
    return sharpness * (1.0 - jnp.tanh(sharpness * (filtered - threshold)) ** 2) / scale_down


def iota(shape, dim):
    return lax.broadcasted_iota(jnp.int32, shape, dim)


def ahead_y(v):
    n = v.ndim
    turned = pltpu.roll(v, LANES - 1, n - 1)
    carried = pltpu.roll(turned, SUBS - 1, n - 2)
    carried = jnp.where(iota(v.shape, n - 2) == SUBS - 1, 0.0, carried)
    return jnp.where(iota(v.shape, n - 1) == LANES - 1, carried, turned)


def behind_y(v):
    n = v.ndim
    turned = pltpu.roll(v, 1, n - 1)
    carried = pltpu.roll(turned, 1, n - 2)
    carried = jnp.where(iota(v.shape, n - 2) == 0, 0.0, carried)
    return jnp.where(iota(v.shape, n - 1) == 0, carried, turned)


def cone(ref, rows):
    table = cone_table(R)
    sums = [ref[:, :, R : R + rows]]
    for a in range(1, R):
        sums.append(ref[:, :, R - a : R - a + rows] + ref[:, :, R + a : R + a + rows])
    blocks = ref.shape[0]
    out = None
    for b in range(R):
        total = None
        for a in range(R):
            if table[a][b] > 0.0:
                term = table[a][b] * sums[a]
                total = term if total is None else total + term
        mid = total[1 : blocks - 1]
        if b == 0:
            out = mid
            continue
        lane = iota(mid.shape, 3)
        upper = jnp.where(lane < b, total[2:], mid)
        lower = jnp.where(lane >= LANES - b, total[: blocks - 2], mid)
        out = out + pltpu.roll(upper, LANES - b, 3) + pltpu.roll(lower, b, 3)
    return out


def kernel(
    gxn,
    gzn,
    fields,
    coef,
    plane_z,
    snap_index,
    fwd_hbm,
    design_hbm,
    sens_hbm,
    out,
    gradient,
    fwd,
    design,
    sens_in,
    E,
    H,
    C,
    exr,
    ezr,
    gxr,
    gzr,
    cxr,
    czr,
    gxs,
    gzs,
    AG,
    DF,
    L,
    SL,
    PT,
    RC,
    WV,
    step_send,
    step_recv,
    ag_send,
    ag_recv,
    rc_send,
    rc_recv,
    row_send,
    row_recv,
    load_sem,
):
    X, Z = coef.shape[0], coef.shape[1]
    NB = coef.shape[2]
    TB = NB // gzn
    WB = TB + 2
    gx, gz = lax.axis_index("gx"), lax.axis_index("gz")
    has_xm, has_xp = gx > 0, gx < gxn - 1
    has_zm, has_zp = gz > 0, gz < gzn - 1

    def load(index, src, dst):
        return pltpu.make_async_copy(src, dst, load_sem.at[index])

    half = X // 2
    loads = [
        load(0, fields.at[0:3, X - 1], E.at[:, X - 1, 0:Z]),
        load(1, fields.at[3:6, X - 1], H.at[:, X, 1 : Z + 1]),
        load(2, fields.at[0:3, 0 : X - 1, Z - 1], E.at[:, 0 : X - 1, Z - 1]),
        load(3, fields.at[3:6, 0 : X - 1, Z - 1], H.at[:, 1:X, Z]),
        load(4, fwd_hbm, fwd),
        load(5, design_hbm, design),
        load(6, sens_hbm, sens_in),
        load(7, fields.at[0:3, 0 : X - 1, 0 : Z - 1], E.at[:, 0 : X - 1, 0 : Z - 1]),
        load(8, fields.at[3:6, 0:half, 0 : Z - 1], H.at[:, 1 : half + 1, 1:Z]),
        load(9, coef.at[0:half], C.at[0:half]),
        load(10, fields.at[3:6, half : X - 1, 0 : Z - 1], H.at[:, half + 1 : X, 1:Z]),
        load(11, coef.at[half:X], C.at[half:X]),
    ]
    for copy in loads:
        copy.start()

    barrier = pltpu.get_barrier_semaphore()

    def greet(x, z):
        pl.semaphore_signal(barrier, inc=1, device_id={"gx": x, "gz": z}, device_id_type=MESH)

    for condition, x, z in (
        (has_xm, gx - 1, gz),
        (has_xp, gx + 1, gz),
        (has_xp & has_zm, gx + 1, gz - 1),
        (has_xm & has_zp, gx - 1, gz + 1),
    ):
        pl.when(condition)(functools.partial(greet, x, z))
    for d in range(1, gzn):
        greet(gx, lax.rem(gz + d, gzn))

    pads = jnp.zeros((2, 2 * PLANES, X, LANES), jnp.float32)
    AG[0:2, DESIGN:] = pads
    AG[NB + 2 :, DESIGN:] = pads
    PT[0] = jnp.zeros(PT.shape[1:], jnp.float32)
    PT[NB + 1] = jnp.zeros(PT.shape[1:], jnp.float32)
    DF[:, :, 0:R] = jnp.zeros((TB + 4, PLANES, R, LANES), jnp.float32)
    DF[:, :, R + X :] = jnp.zeros((TB + 4, PLANES, R, LANES), jnp.float32)

    E[:, X] = jnp.zeros((COMPS, Z + 1, SUBS, LANES), jnp.float32)
    E[:, 0:X, Z] = jnp.zeros((COMPS, X, SUBS, LANES), jnp.float32)
    H[:, 0] = jnp.zeros((COMPS, Z + 1, SUBS, LANES), jnp.float32)
    H[:, 1:, 0] = jnp.zeros((COMPS, X, SUBS, LANES), jnp.float32)

    met = (
        has_xm.astype(jnp.int32)
        + has_xp.astype(jnp.int32)
        + (has_xp & has_zm).astype(jnp.int32)
        + (has_xm & has_zp).astype(jnp.int32)
        + (gzn - 1)
    )
    pl.semaphore_wait(barrier, met)

    def remote(src, dst, send, recv, x, z):
        return pltpu.make_async_remote_copy(
            src_ref=src,
            dst_ref=dst,
            send_sem=send,
            recv_sem=recv,
            device_id={"gx": x, "gz": z},
            device_id_type=MESH,
        )

    def step_copies(s):
        electric = fields if s == 0 else E

        def make(k, src, dst, x, z):
            return remote(src, dst, step_send.at[s, k], step_recv.at[s, k], x, z)

        return dict(
            ex=(make(0, electric.at[1:3, 0, 0:Z], exr.at[s], gx - 1, gz), has_xm, has_xp),
            ez=(make(1, electric.at[0:2, 0:X, 0], ezr.at[s], gx, gz - 1), has_zm, has_zp),
            cx=(
                make(2, electric.at[0, X - 1, 0], cxr.at[s], gx + 1, gz - 1),
                has_xp & has_zm,
                has_xm & has_zp,
            ),
            cz=(
                make(3, electric.at[2, 0, Z - 1], czr.at[s], gx - 1, gz + 1),
                has_xm & has_zp,
                has_xp & has_zm,
            ),
            gx=(make(4, gxs.at[s], gxr.at[s], gx + 1, gz), has_xp, has_xm),
            gz=(make(5, gzs.at[s], gzr.at[s], gx, gz + 1), has_zp, has_zm),
        )

    def start(item):
        pl.when(item[1])(item[0].start)

    def finish_send(item):
        pl.when(item[1])(item[0].wait_send)

    def fill_sends(s):
        E[0, X - 1, Z] = jnp.zeros((SUBS, LANES), jnp.float32)
        E[2, X, Z - 1] = jnp.zeros((SUBS, LANES), jnp.float32)
        ex, ey, ez = (E[c, X - 1, 0:Z] for c in range(3))
        gxs[s, 0] = H[1, X, 1:] + magnetic_step * (E[0, X - 1, 1 : Z + 1] - ex + ez)
        gxs[s, 1] = H[2, X, 1:] - magnetic_step * (ey + ahead_y(ex) - ex)
        ex, ey, ez = (E[c, 0:X, Z - 1] for c in range(3))
        gzs[s, 0] = H[0, 1:, Z] + magnetic_step * (ahead_y(ez) - ez + ey)
        gzs[s, 1] = H[1, 1:, Z] - magnetic_step * (ex + E[2, 1 : X + 1, Z - 1] - ez)

    def receive(s, copies):
        @pl.when(has_xp)
        def _():
            copies["ex"][0].wait_recv()
            E[1:3, X, 0:Z] = exr[s]

        @pl.when(has_zp)
        def _():
            copies["ez"][0].wait_recv()
            E[0:2, 0:X, Z] = ezr[s]

        @pl.when(has_xm)
        def _():
            copies["gx"][0].wait_recv()
            H[1, 0, 1:] = gxr[s, 0] - magnetic_step * E[2, 0, 0:Z]
            H[2, 0, 1:] = gxr[s, 1] + magnetic_step * E[1, 0, 0:Z]

        @pl.when(has_zm)
        def _():
            copies["gz"][0].wait_recv()
            H[0, 1:, 0] = gzr[s, 0] - magnetic_step * E[1, 0:X, 0]
            H[1, 1:, 0] = gzr[s, 1] + magnetic_step * E[0, 0:X, 0]

        @pl.when(has_xm & has_zp)
        def _():
            copies["cx"][0].wait_recv()
            H[1, 0, Z] = H[1, 0, Z] + magnetic_step * cxr[s]

        @pl.when(has_xp & has_zm)
        def _():
            copies["cz"][0].wait_recv()
            H[1, X, 0] = H[1, X, 0] - magnetic_step * czr[s]

    def curl_h(e, next_x, next_z):
        (ex, ey, ez), (ey_x, ez_x), (ex_z, ey_z) = e, next_x, next_z
        return (
            magnetic_step * ((ahead_y(ez) - ez) - (ey_z - ey)),
            magnetic_step * ((ex_z - ex) - (ez_x - ez)),
            magnetic_step * ((ey_x - ey) - (ahead_y(ex) - ex)),
        )

    def new_e(e, h, before_x, before_z, factor):
        (hx, hy, hz), (hy_x, hz_x), (hx_z, hy_z) = h, before_x, before_z
        return (
            e[0] - factor * ((hz - behind_y(hz)) - (hy - hy_z)),
            e[1] - factor * ((hx - hx_z) - (hz - hz_x)),
            e[2] - factor * ((hy - hy_x) - (hx - behind_y(hx))),
        )

    def sweep(s, x_start, x_stop, width=4):
        @pl.loop(x_start, x_stop)
        def _(x):
            below = (H[0, x + 1, 0:1], H[1, x + 1, 0:1])
            for z in range(0, Z, width):
                own, up = slice(z, z + width), slice(z + 1, z + width + 1)
                ex, ey = E[0, x, z : z + width + 1], E[1, x, z : z + width + 1]
                e = (ex[:-1], ey[:-1], E[2, x, own])
                curl = curl_h(e, (E[1, x + 1, own], E[2, x + 1, own]), (ex[1:], ey[1:]))
                h = tuple(H[c, x + 1, up] + curl[c] for c in range(COMPS))
                before_z = tuple(
                    jnp.concatenate([first, value[:-1]], axis=0) for first, value in zip(below, h)
                )
                below = (h[0][-1:], h[1][-1:])
                e = new_e(e, h, (H[1, x, up], H[2, x, up]), before_z, C[x, own])
                H[1, x + 1, up], H[2, x + 1, up] = h[1], h[2]
                if s + 1 < STEPS:
                    H[0, x + 1, up] = h[0]
                    for c in range(COMPS):
                        E[c, x, own] = e[c]
                else:
                    for c in range(COMPS):
                        out[c, x, own] = e[c]
                        out[COMPS + c, x, own] = h[c]

    def layer_of(p):
        local = plane_z[p] - gz * Z
        inside = (local >= 0) & (local < Z)
        return jnp.clip(local, 0, Z - 1), jnp.where(inside, 1.0, 0.0).astype(jnp.float32)

    def products(step):
        @pl.loop(0, NB)
        def _(block):
            for p in range(PLANES):
                total = None
                for c in range(COMPS):
                    image = (step * PLANES + p) * COMPS + c
                    term = AG[block + 2, image] * L[step, p, c, :, block]
                    total = term if total is None else total + term
                if step:
                    total = PT[block + 1, p] + total
                PT[block + 1, p] = total

    def plane_e(layer):
        def h_at(z):
            e = tuple(E[c, 0:X, z] for c in range(COMPS))
            curl = curl_h(
                e, (E[1, 1 : X + 1, z], E[2, 1 : X + 1, z]), (E[0, 0:X, z + 1], E[1, 0:X, z + 1])
            )
            return e, tuple(H[c, 1 : X + 1, z + 1] + curl[c] for c in range(COMPS))

        e, h = h_at(layer)
        _, under = h_at(jnp.maximum(layer - 1, 0))
        lowest = layer == 0
        before_z = tuple(jnp.where(lowest, H[c, 1 : X + 1, 0], under[c]) for c in range(2))
        before_x = tuple(
            jnp.concatenate([H[c, 0:1, layer + 1], h[c][:-1]], axis=0) for c in (1, 2)
        )
        return new_e(e, h, before_x, before_z, C[0:X, layer])

    copies = step_copies(0)
    for name in ("ex", "ez", "cx", "cz"):
        start(copies[name])
    for copy in loads[:4]:
        copy.wait()
    fill_sends(0)
    start(copies["gx"])
    start(copies["gz"])
    for copy in loads[4:7]:
        copy.wait()
    snap = snap_index[0]
    for block in range(TB):
        lanes = slice(block * LANES, (block + 1) * LANES)
        place = 2 + gz * TB + block
        for step in range(STEPS):
            for p in range(PLANES):
                for c in range(COMPS):
                    AG[place, (step * PLANES + p) * COMPS + c] = fwd[snap + step, p, c, :, lanes]
        AG[place, DESIGN:SENS] = design[:, :, lanes]
        AG[place, SENS:] = sens_in[:, :, lanes]
    tile = pl.ds(2 + gz * TB, TB)
    gathers = [
        remote(AG.at[tile], AG.at[tile], ag_send.at[d], ag_recv.at[d], gx, lax.rem(gz + d, gzn))
        for d in range(1, gzn)
    ]
    for copy in gathers:
        copy.start()
    for copy in loads[7:10]:
        copy.wait()
    receive(0, copies)
    sweep(0, 0, half)
    for copy in loads[10:]:
        copy.wait()
    sweep(0, half, X)
    for item in copies.values():
        finish_send(item)

    copies = step_copies(1)
    for name in ("ex", "ez", "cx", "cz"):
        start(copies[name])
    fill_sends(1)
    start(copies["gx"])
    start(copies["gz"])
    for p in range(PLANES):
        layer, inside = layer_of(p)
        for c in range(COMPS):
            L[0, p, c] = E[c, 0:X, layer] * inside
    for d in range(1, gzn):
        source = pl.ds(2 + lax.rem(gz + gzn - d, gzn) * TB, TB)
        remote(
            AG.at[tile], AG.at[source], ag_send.at[d], ag_recv.at[d], gx, lax.rem(gz + d, gzn)
        ).wait_recv()
    around = pl.ds(gz * TB, TB + 4)
    rows = [
        (
            remote(
                AG.at[around, DESIGN:SENS, X - R : X],
                DF.at[:, :, 0:R],
                row_send.at[0],
                row_recv.at[0],
                gx + 1,
                gz,
            ),
            has_xp,
            has_xm,
        ),
        (
            remote(
                AG.at[around, DESIGN:SENS, 0:R],
                DF.at[:, :, R + X : X + 2 * R],
                row_send.at[1],
                row_recv.at[1],
                gx - 1,
                gz,
            ),
            has_xm,
            has_xp,
        ),
    ]
    for item in rows:
        start(item)
    products(0)

    DF[:, :, R : R + X] = AG[around, DESIGN:SENS]
    for item in rows:
        pl.when(item[2])(item[0].wait_recv)
    SL[...] = projection_slope(cone(DF, X))
    receive(1, copies)

    for p in range(PLANES):
        layer, inside = layer_of(p)
        for c, value in enumerate(plane_e(layer)):
            L[1, p, c] = value * inside
    products(1)
    partials = []
    for d in range(1, gzn):
        peer = lax.rem(gz + d, gzn)
        partials.append(
            remote(
                PT.at[pl.ds(peer * TB, WB)],
                RC.at[d],
                rc_send.at[d],
                rc_recv.at[d],
                gx,
                peer,
            )
        )
    for copy in partials:
        copy.start()
    sweep(1, 0, X)
    total = AG[pl.ds(gz * TB + 1, WB), SENS:] + PT[pl.ds(gz * TB, WB)]
    for d, copy in enumerate(partials, 1):
        copy.wait_recv()
        total = total + RC[d]
    WV[:, :, R : R + X] = total * SL[...]
    edges = [
        (
            remote(
                WV.at[:, :, X : X + R], WV.at[:, :, 0:R], row_send.at[2], row_recv.at[2], gx + 1, gz
            ),
            has_xp,
            has_xm,
        ),
        (
            remote(
                WV.at[:, :, R : 2 * R],
                WV.at[:, :, R + X : X + 2 * R],
                row_send.at[3],
                row_recv.at[3],
                gx - 1,
                gz,
            ),
            has_xm,
            has_xp,
        ),
    ]
    for item in edges:
        start(item)
    none = jnp.zeros((WB, PLANES, R, LANES), jnp.float32)

    @pl.when(gx == 0)
    def _():
        WV[:, :, 0:R] = none

    @pl.when(gx == gxn - 1)
    def _():
        WV[:, :, R + X :] = none

    for item in edges:
        pl.when(item[2])(item[0].wait_recv)
    result = cone(WV, X)
    for block in range(TB):
        gradient[:, :, block * LANES : (block + 1) * LANES] = result[block]

    for copy in gathers + partials:
        copy.wait_send()
    for item in rows + edges + list(copies.values()):
        finish_send(item)


def shards(adj_fields, coef_e, plane_z, snap_index, fwd_snaps, design, sens_in):
    gxn, gzn = lax.axis_size("gx"), lax.axis_size("gz")
    X, Z, NB = coef_e.shape[0], coef_e.shape[1], coef_e.shape[2]
    TB = NB // gzn
    WB = TB + 2
    cell = (SUBS, LANES)

    def vmem(*shape):
        return pltpu.VMEM(shape, jnp.float32)

    hbm = pl.BlockSpec(memory_space=pltpu.HBM)
    smem = pl.BlockSpec(memory_space=pltpu.SMEM)
    local = pl.BlockSpec(memory_space=pltpu.VMEM)
    dma = pltpu.SemaphoreType.DMA
    return pl.pallas_call(
        functools.partial(kernel, gxn, gzn),
        out_shape=(
            pltpu.VMEM(adj_fields.shape, jnp.float32),
            pltpu.VMEM(design.shape, jnp.float32),
        ),
        in_specs=[hbm, hbm, smem, smem, hbm, hbm, hbm],
        out_specs=(local, local),
        scratch_shapes=[
            vmem(*fwd_snaps.shape),
            vmem(*design.shape),
            vmem(*sens_in.shape),
            vmem(COMPS, X + 1, Z + 1, *cell),
            vmem(COMPS, X + 1, Z + 1, *cell),
            vmem(X, Z, *cell),
            vmem(STEPS, 2, Z, *cell),
            vmem(STEPS, 2, X, *cell),
            vmem(STEPS, 2, Z, *cell),
            vmem(STEPS, 2, X, *cell),
            vmem(STEPS, *cell),
            vmem(STEPS, *cell),
            vmem(STEPS, 2, Z, *cell),
            vmem(STEPS, 2, X, *cell),
            vmem(NB + 4, IMAGES, X, LANES),
            vmem(TB + 4, PLANES, X + 2 * R, LANES),
            vmem(STEPS, PLANES, COMPS, X, *cell),
            vmem(WB, PLANES, X, LANES),
            vmem(NB + 2, PLANES, X, LANES),
            vmem(gzn, WB, PLANES, X, LANES),
            vmem(WB, PLANES, X + 2 * R, LANES),
            dma((STEPS, 6)),
            dma((STEPS, 6)),
            dma((gzn,)),
            dma((gzn,)),
            dma((gzn,)),
            dma((gzn,)),
            dma((4,)),
            dma((4,)),
            dma((12,)),
        ],
        compiler_params=pltpu.CompilerParams(
            collective_id=0, has_side_effects=True, vmem_limit_bytes=51 * 2**20
        ),
    )(adj_fields, coef_e, plane_z, snap_index, fwd_snaps, design, sens_in)


def solution(mesh):
    in_specs = (
        P(None, "gx", "gz", None, None),
        P("gx", "gz", None, None),
        P(),
        P(),
        P(None, None, None, "gx", "gz"),
        P(None, "gx", "gz"),
        P(None, "gx", "gz"),
    )
    out_specs = (P(None, "gx", "gz", None, None), P(None, "gx", "gz"))
    return jax.shard_map(shards, mesh=mesh, in_specs=in_specs, out_specs=out_specs, check_vma=False)
```

```python
import functools
import math

import jax
import jax.numpy as jnp
from jax import lax
from jax.experimental import pallas as pl
from jax.experimental.pallas import tpu as pltpu
from jax.sharding import PartitionSpec as P

R = 8
STEPS = 2
PLANES = 2
COMPS = 3
LANES = 128
SUBS = 8

magnetic_step = 0.5
sharpness = 8.0
threshold = 0.5

MESH = pl.DeviceIdType.MESH


def cone_table(radius):
    raw = [
        [max(0.0, radius - math.sqrt(a * a + b * b)) for b in range(radius + 1)]
        for a in range(radius + 1)
    ]
    total = sum(
        raw[abs(a)][abs(b)]
        for a in range(-radius, radius + 1)
        for b in range(-radius, radius + 1)
    )
    return [[entry / total for entry in line] for line in raw]


def projection_slope(filtered):
    scale_down = math.tanh(sharpness * threshold) + math.tanh(sharpness * (1.0 - threshold))
    return sharpness * (1.0 - jnp.tanh(sharpness * (filtered - threshold)) ** 2) / scale_down


def iota(shape, dim):
    return lax.broadcasted_iota(jnp.int32, shape, dim)


def ahead_y(v):
    n = v.ndim
    turned = pltpu.roll(v, LANES - 1, n - 1)
    carried = pltpu.roll(turned, SUBS - 1, n - 2)
    carried = jnp.where(iota(v.shape, n - 2) == SUBS - 1, 0.0, carried)
    return jnp.where(iota(v.shape, n - 1) == LANES - 1, carried, turned)


def behind_y(v):
    n = v.ndim
    turned = pltpu.roll(v, 1, n - 1)
    carried = pltpu.roll(turned, 1, n - 2)
    carried = jnp.where(iota(v.shape, n - 2) == 0, 0.0, carried)
    return jnp.where(iota(v.shape, n - 1) == 0, carried, turned)


def cone(ref, rows):
    table = cone_table(R)
    sums = [ref[:, :, R : R + rows]]
    for a in range(1, R):
        sums.append(ref[:, :, R - a : R - a + rows] + ref[:, :, R + a : R + a + rows])
    blocks = ref.shape[0]
    out = None
    for b in range(R):
        total = None
        for a in range(R):
            if table[a][b] > 0.0:
                term = table[a][b] * sums[a]
                total = term if total is None else total + term
        mid = total[1 : blocks - 1]
        if b == 0:
            out = mid
            continue
        lane = iota(mid.shape, 3)
        upper = jnp.where(lane < b, total[2:], mid)
        lower = jnp.where(lane >= LANES - b, total[: blocks - 2], mid)
        out = out + pltpu.roll(upper, LANES - b, 3) + pltpu.roll(lower, b, 3)
    return out


def kernel(
    gxn,
    gzn,
    fields,
    coef,
    plane_z,
    snap_index,
    fwd_hbm,
    design_hbm,
    sens_hbm,
    out,
    gradient,
    fwd,
    sens_in,
    E,
    H,
    C,
    exr,
    ezr,
    gxr,
    gzr,
    cxr,
    czr,
    gxs,
    gzs,
    DF,
    L,
    LB,
    LR,
    SL,
    WV,
    step_send,
    step_recv,
    layer_send,
    layer_recv,
    tile_send,
    tile_recv,
    load_sem,
):
    X, Z = coef.shape[0], coef.shape[1]
    NB = coef.shape[2]
    TB = NB // gzn
    gx, gz = lax.axis_index("gx"), lax.axis_index("gz")
    has_xm, has_xp = gx > 0, gx < gxn - 1
    has_zm, has_zp = gz > 0, gz < gzn - 1

    DF[...] = jnp.zeros(DF.shape, jnp.float32)
    WV[...] = jnp.zeros(WV.shape, jnp.float32)

    def load(index, src, dst):
        return pltpu.make_async_copy(src, dst, load_sem.at[index])

    half = X // 2
    loads = [
        load(0, fields.at[0:3, X - 1], E.at[:, X - 1, 0:Z]),
        load(1, fields.at[3:6, X - 1], H.at[:, X, 1 : Z + 1]),
        load(2, fields.at[0:3, 0 : X - 1, Z - 1], E.at[:, 0 : X - 1, Z - 1]),
        load(3, fields.at[3:6, 0 : X - 1, Z - 1], H.at[:, 1:X, Z]),
        load(4, fields.at[0:3, 0 : X - 1, 0 : Z - 1], E.at[:, 0 : X - 1, 0 : Z - 1]),
        load(5, fields.at[3:6, 0:half, 0 : Z - 1], H.at[:, 1 : half + 1, 1:Z]),
        load(6, coef.at[0:half], C.at[0:half]),
        load(7, fields.at[3:6, half : X - 1, 0 : Z - 1], H.at[:, half + 1 : X, 1:Z]),
        load(8, coef.at[half:X], C.at[half:X]),
        load(9, fwd_hbm, fwd),
        load(10, sens_hbm, sens_in),
    ]
    designs = [
        load(
            11 + block,
            design_hbm.at[:, :, block * LANES : (block + 1) * LANES],
            DF.at[1 + block, :, R : R + X],
        )
        for block in range(TB)
    ]
    for copy in loads[:4] + designs + loads[4:]:
        copy.start()

    barrier = pltpu.get_barrier_semaphore()

    def greet(x, z):
        pl.semaphore_signal(barrier, inc=1, device_id={"gx": x, "gz": z}, device_id_type=MESH)

    for condition, x, z in (
        (has_xm, gx - 1, gz),
        (has_xp, gx + 1, gz),
        (has_xp & has_zm, gx + 1, gz - 1),
        (has_xm & has_zp, gx - 1, gz + 1),
        (has_xp & has_zp, gx + 1, gz + 1),
        (has_xm & has_zm, gx - 1, gz - 1),
    ):
        pl.when(condition)(functools.partial(greet, x, z))
    for d in range(1, gzn):
        greet(gx, lax.rem(gz + d, gzn))

    E[:, X] = jnp.zeros((COMPS, Z + 1, SUBS, LANES), jnp.float32)
    E[:, 0:X, Z] = jnp.zeros((COMPS, X, SUBS, LANES), jnp.float32)
    H[:, 0] = jnp.zeros((COMPS, Z + 1, SUBS, LANES), jnp.float32)
    H[:, 1:, 0] = jnp.zeros((COMPS, X, SUBS, LANES), jnp.float32)

    met = (
        has_xm.astype(jnp.int32)
        + has_xp.astype(jnp.int32)
        + (has_xp & has_zm).astype(jnp.int32)
        + (has_xm & has_zp).astype(jnp.int32)
        + (has_xp & has_zp).astype(jnp.int32)
        + (has_xm & has_zm).astype(jnp.int32)
        + (gzn - 1)
    )
    pl.semaphore_wait(barrier, met)

    def remote(src, dst, send, recv, x, z):
        return pltpu.make_async_remote_copy(
            src_ref=src,
            dst_ref=dst,
            send_sem=send,
            recv_sem=recv,
            device_id={"gx": x, "gz": z},
            device_id_type=MESH,
        )

    def step_copies(s):
        electric = fields if s == 0 else E

        def make(k, src, dst, x, z):
            return remote(src, dst, step_send.at[s, k], step_recv.at[s, k], x, z)

        return dict(
            ex=(make(0, electric.at[1:3, 0, 0:Z], exr.at[s], gx - 1, gz), has_xm, has_xp),
            ez=(make(1, electric.at[0:2, 0:X, 0], ezr.at[s], gx, gz - 1), has_zm, has_zp),
            cx=(
                make(2, electric.at[0, X - 1, 0], cxr.at[s], gx + 1, gz - 1),
                has_xp & has_zm,
                has_xm & has_zp,
            ),
            cz=(
                make(3, electric.at[2, 0, Z - 1], czr.at[s], gx - 1, gz + 1),
                has_xm & has_zp,
                has_xp & has_zm,
            ),
            gx=(make(4, gxs.at[s], gxr.at[s], gx + 1, gz), has_xp, has_xm),
            gz=(make(5, gzs.at[s], gzr.at[s], gx, gz + 1), has_zp, has_zm),
        )

    def tile_copies(first, ref):
        has = {(-1, 0): has_xm, (1, 0): has_xp, (0, -1): has_zm, (0, 1): has_zp}
        row_from = {0: slice(R, R + X), 1: slice(X, X + R), -1: slice(R, 2 * R)}
        row_to = {0: slice(R, R + X), 1: slice(0, R), -1: slice(R + X, X + 2 * R)}
        block_from = {0: slice(1, TB + 1), 1: slice(TB, TB + 1), -1: slice(1, 2)}
        block_to = {0: slice(1, TB + 1), 1: slice(0, 1), -1: slice(TB + 1, TB + 2)}

        def exists(dx, dz):
            if not dz:
                return has[dx, 0]
            return has[0, dz] if not dx else has[dx, 0] & has[0, dz]

        items = []
        for dx in (0, 1, -1):
            for dz in (0, 1, -1):
                if not (dx or dz):
                    continue
                k = first + len(items)
                copy = remote(
                    ref.at[block_from[dz], :, row_from[dx]],
                    ref.at[block_to[dz], :, row_to[dx]],
                    tile_send.at[k],
                    tile_recv.at[k],
                    gx + dx,
                    gz + dz,
                )
                items.append((copy, exists(dx, dz), exists(-dx, -dz)))
        return items

    def layer_copies(s):
        copies = []
        for d in range(1, gzn):
            peer = lax.rem(gz + d, gzn)
            copies.append(
                remote(
                    LB.at[s, pl.ds(peer * TB, TB)],
                    LR.at[s, d],
                    layer_send.at[s, d],
                    layer_recv.at[s, d],
                    gx,
                    peer,
                )
            )
        return copies

    def start(item):
        pl.when(item[1])(item[0].start)

    def finish_send(item):
        pl.when(item[1])(item[0].wait_send)

    def fill_sends(s):
        E[0, X - 1, Z] = jnp.zeros((SUBS, LANES), jnp.float32)
        E[2, X, Z - 1] = jnp.zeros((SUBS, LANES), jnp.float32)
        ex, ey, ez = (E[c, X - 1, 0:Z] for c in range(3))
        gxs[s, 0] = H[1, X, 1:] + magnetic_step * (E[0, X - 1, 1 : Z + 1] - ex + ez)
        gxs[s, 1] = H[2, X, 1:] - magnetic_step * (ey + ahead_y(ex) - ex)
        ex, ey, ez = (E[c, 0:X, Z - 1] for c in range(3))
        gzs[s, 0] = H[0, 1:, Z] + magnetic_step * (ahead_y(ez) - ez + ey)
        gzs[s, 1] = H[1, 1:, Z] - magnetic_step * (ex + E[2, 1 : X + 1, Z - 1] - ez)

    def receive(s, copies):
        @pl.when(has_xp)
        def _():
            copies["ex"][0].wait_recv()
            E[1:3, X, 0:Z] = exr[s]

        @pl.when(has_zp)
        def _():
            copies["ez"][0].wait_recv()
            E[0:2, 0:X, Z] = ezr[s]

        @pl.when(has_xm)
        def _():
            copies["gx"][0].wait_recv()
            H[1, 0, 1:] = gxr[s, 0] - magnetic_step * E[2, 0, 0:Z]
            H[2, 0, 1:] = gxr[s, 1] + magnetic_step * E[1, 0, 0:Z]

        @pl.when(has_zm)
        def _():
            copies["gz"][0].wait_recv()
            H[0, 1:, 0] = gzr[s, 0] - magnetic_step * E[1, 0:X, 0]
            H[1, 1:, 0] = gzr[s, 1] + magnetic_step * E[0, 0:X, 0]

        @pl.when(has_xm & has_zp)
        def _():
            copies["cx"][0].wait_recv()
            H[1, 0, Z] = H[1, 0, Z] + magnetic_step * cxr[s]

        @pl.when(has_xp & has_zm)
        def _():
            copies["cz"][0].wait_recv()
            H[1, X, 0] = H[1, X, 0] - magnetic_step * czr[s]

    def curl_h(e, next_x, next_z):
        (ex, ey, ez), (ey_x, ez_x), (ex_z, ey_z) = e, next_x, next_z
        return (
            magnetic_step * ((ahead_y(ez) - ez) - (ey_z - ey)),
            magnetic_step * ((ex_z - ex) - (ez_x - ez)),
            magnetic_step * ((ey_x - ey) - (ahead_y(ex) - ex)),
        )

    def new_e(e, h, before_x, before_z, factor):
        (hx, hy, hz), (hy_x, hz_x), (hx_z, hy_z) = h, before_x, before_z
        return (
            e[0] - factor * ((hz - behind_y(hz)) - (hy - hy_z)),
            e[1] - factor * ((hx - hx_z) - (hz - hz_x)),
            e[2] - factor * ((hy - hy_x) - (hx - behind_y(hx))),
        )

    def sweep(s, x_start, x_stop, width=4):
        @pl.loop(x_start, x_stop)
        def _(x):
            below = (H[0, x + 1, 0:1], H[1, x + 1, 0:1])
            for z in range(0, Z, width):
                own, up = slice(z, z + width), slice(z + 1, z + width + 1)
                ex, ey = E[0, x, z : z + width + 1], E[1, x, z : z + width + 1]
                e = (ex[:-1], ey[:-1], E[2, x, own])
                curl = curl_h(e, (E[1, x + 1, own], E[2, x + 1, own]), (ex[1:], ey[1:]))
                h = tuple(H[c, x + 1, up] + curl[c] for c in range(COMPS))
                before_z = tuple(
                    jnp.concatenate([first, value[:-1]], axis=0) for first, value in zip(below, h)
                )
                below = (h[0][-1:], h[1][-1:])
                e = new_e(e, h, (H[1, x, up], H[2, x, up]), before_z, C[x, own])
                H[1, x + 1, up], H[2, x + 1, up] = h[1], h[2]
                if s + 1 < STEPS:
                    H[0, x + 1, up] = h[0]
                    for c in range(COMPS):
                        E[c, x, own] = e[c]
                else:
                    for c in range(COMPS):
                        out[c, x, own] = e[c]
                        out[COMPS + c, x, own] = h[c]

    def layer_of(p):
        local = plane_z[p] - gz * Z
        inside = (local >= 0) & (local < Z)
        return jnp.clip(local, 0, Z - 1), jnp.where(inside, 1.0, 0.0).astype(jnp.float32)

    def send_layers(s, new_layers):
        for p in range(PLANES):
            layer, inside = layer_of(p)
            for c, value in enumerate(new_layers(layer)):
                L[s, p, c] = value * inside
        for block in range(NB):
            for p in range(PLANES):
                for c in range(COMPS):
                    LB[s, block, p * COMPS + c] = L[s, p, c, :, block]
        copies = layer_copies(s)
        for copy in copies:
            copy.start()
        return copies

    def plane_e(layer):
        def h_at(z):
            e = tuple(E[c, 0:X, z] for c in range(COMPS))
            curl = curl_h(
                e, (E[1, 1 : X + 1, z], E[2, 1 : X + 1, z]), (E[0, 0:X, z + 1], E[1, 0:X, z + 1])
            )
            return e, tuple(H[c, 1 : X + 1, z + 1] + curl[c] for c in range(COMPS))

        e, h = h_at(layer)
        _, under = h_at(jnp.maximum(layer - 1, 0))
        lowest = layer == 0
        before_z = tuple(jnp.where(lowest, H[c, 1 : X + 1, 0], under[c]) for c in range(2))
        before_x = tuple(
            jnp.concatenate([H[c, 0:1, layer + 1], h[c][:-1]], axis=0) for c in (1, 2)
        )
        return new_e(e, h, before_x, before_z, C[0:X, layer])

    copies = step_copies(0)
    for name in ("ex", "ez", "cx", "cz"):
        start(copies[name])
    for copy in loads[:4]:
        copy.wait()
    fill_sends(0)
    start(copies["gx"])
    start(copies["gz"])
    for copy in designs:
        copy.wait()
    design_edges = tile_copies(0, DF)
    for item in design_edges:
        start(item)
    for copy in loads[4:7]:
        copy.wait()
    receive(0, copies)
    sweep(0, 0, half)
    for copy in loads[7:]:
        copy.wait()
    sweep(0, half, X)
    for item in copies.values():
        finish_send(item)

    copies = step_copies(1)
    for name in ("ex", "ez", "cx", "cz"):
        start(copies[name])
    fill_sends(1)
    start(copies["gx"])
    start(copies["gz"])
    layers = send_layers(0, lambda z: tuple(E[c, 0:X, z] for c in range(COMPS)))

    for item in design_edges:
        pl.when(item[2])(item[0].wait_recv)
    SL[...] = projection_slope(cone(DF, X))
    receive(1, copies)

    layers += send_layers(1, plane_e)
    sweep(1, 0, X)

    for copy in layers:
        copy.wait_recv()
    snap = snap_index[0]
    for block in range(TB):
        lanes = slice(block * LANES, (block + 1) * LANES)
        total = sens_in[:, :, lanes]
        for step in range(STEPS):
            electric = LB[step, gz * TB + block]
            for d in range(1, gzn):
                electric = electric + LR[step, d, block]
            electric = electric.reshape(PLANES, COMPS, X, LANES)
            total = total + jnp.sum(fwd[snap + step, :, :, :, lanes] * electric, axis=1)
        WV[1 + block, :, R : R + X] = total * SL[block]
    weighted_edges = tile_copies(8, WV)
    for item in weighted_edges:
        start(item)
    for item in weighted_edges:
        pl.when(item[2])(item[0].wait_recv)
    result = cone(WV, X)
    for block in range(TB):
        gradient[:, :, block * LANES : (block + 1) * LANES] = result[block]

    for copy in layers:
        copy.wait_send()
    for item in design_edges + weighted_edges + list(copies.values()):
        finish_send(item)


def shards(adj_fields, coef_e, plane_z, snap_index, fwd_snaps, design, sens_in):
    gxn, gzn = lax.axis_size("gx"), lax.axis_size("gz")
    X, Z, NB = coef_e.shape[0], coef_e.shape[1], coef_e.shape[2]
    TB = NB // gzn
    cell = (SUBS, LANES)

    def vmem(*shape):
        return pltpu.VMEM(shape, jnp.float32)

    hbm = pl.BlockSpec(memory_space=pltpu.HBM)
    smem = pl.BlockSpec(memory_space=pltpu.SMEM)
    local = pl.BlockSpec(memory_space=pltpu.VMEM)
    dma = pltpu.SemaphoreType.DMA
    return pl.pallas_call(
        functools.partial(kernel, gxn, gzn),
        out_shape=(
            pltpu.VMEM(adj_fields.shape, jnp.float32),
            pltpu.VMEM(design.shape, jnp.float32),
        ),
        in_specs=[hbm, hbm, smem, smem, hbm, hbm, hbm],
        out_specs=(local, local),
        scratch_shapes=[
            vmem(*fwd_snaps.shape),
            vmem(*sens_in.shape),
            vmem(COMPS, X + 1, Z + 1, *cell),
            vmem(COMPS, X + 1, Z + 1, *cell),
            vmem(X, Z, *cell),
            vmem(STEPS, 2, Z, *cell),
            vmem(STEPS, 2, X, *cell),
            vmem(STEPS, 2, Z, *cell),
            vmem(STEPS, 2, X, *cell),
            vmem(STEPS, *cell),
            vmem(STEPS, *cell),
            vmem(STEPS, 2, Z, *cell),
            vmem(STEPS, 2, X, *cell),
            vmem(TB + 2, PLANES, X + 2 * R, LANES),
            vmem(STEPS, PLANES, COMPS, X, *cell),
            vmem(STEPS, NB, PLANES * COMPS, X, LANES),
            vmem(STEPS, gzn, TB, PLANES * COMPS, X, LANES),
            vmem(TB, PLANES, X, LANES),
            vmem(TB + 2, PLANES, X + 2 * R, LANES),
            dma((STEPS, 6)),
            dma((STEPS, 6)),
            dma((STEPS, gzn)),
            dma((STEPS, gzn)),
            dma((16,)),
            dma((16,)),
            dma((11 + TB,)),
        ],
        compiler_params=pltpu.CompilerParams(
            collective_id=0, has_side_effects=True, vmem_limit_bytes=51 * 2**20
        ),
    )(adj_fields, coef_e, plane_z, snap_index, fwd_snaps, design, sens_in)


def solution(mesh):
    in_specs = (
        P(None, "gx", "gz", None, None),
        P("gx", "gz", None, None),
        P(),
        P(),
        P(None, None, None, "gx", "gz"),
        P(None, "gx", "gz"),
        P(None, "gx", "gz"),
    )
    out_specs = (P(None, "gx", "gz", None, None), P(None, "gx", "gz"))
    return jax.shard_map(shards, mesh=mesh, in_specs=in_specs, out_specs=out_specs, check_vma=False)
```

```python
import functools
import math

import jax
import jax.numpy as jnp
from jax import lax
from jax.experimental import pallas as pl
from jax.experimental.pallas import tpu as pltpu
from jax.sharding import PartitionSpec as P

R = 8
STEPS = 2
PLANES = 2
COMPS = 3
IMAGES = STEPS * PLANES * COMPS + 2 * PLANES
DESIGN = STEPS * PLANES * COMPS
SENS = DESIGN + PLANES
LANES = 128
SUBS = 8

magnetic_step = 0.5
sharpness = 8.0
threshold = 0.5

MESH = pl.DeviceIdType.MESH


def cone_table(radius):
    raw = [
        [max(0.0, radius - math.sqrt(a * a + b * b)) for b in range(radius + 1)]
        for a in range(radius + 1)
    ]
    total = sum(
        raw[abs(a)][abs(b)]
        for a in range(-radius, radius + 1)
        for b in range(-radius, radius + 1)
    )
    return [[entry / total for entry in line] for line in raw]


def projection_slope(filtered):
    scale_down = math.tanh(sharpness * threshold) + math.tanh(sharpness * (1.0 - threshold))
    return sharpness * (1.0 - jnp.tanh(sharpness * (filtered - threshold)) ** 2) / scale_down


def iota(shape, dim):
    return lax.broadcasted_iota(jnp.int32, shape, dim)


def ahead_y(v):
    n = v.ndim
    turned = pltpu.roll(v, LANES - 1, n - 1)
    carried = pltpu.roll(turned, SUBS - 1, n - 2)
    carried = jnp.where(iota(v.shape, n - 2) == SUBS - 1, 0.0, carried)
    return jnp.where(iota(v.shape, n - 1) == LANES - 1, carried, turned)


def behind_y(v):
    n = v.ndim
    turned = pltpu.roll(v, 1, n - 1)
    carried = pltpu.roll(turned, 1, n - 2)
    carried = jnp.where(iota(v.shape, n - 2) == 0, 0.0, carried)
    return jnp.where(iota(v.shape, n - 1) == 0, carried, turned)


def cone(ref, rows):
    table = cone_table(R)
    sums = [ref[:, :, R : R + rows]]
    for a in range(1, R):
        sums.append(ref[:, :, R - a : R - a + rows] + ref[:, :, R + a : R + a + rows])
    blocks = ref.shape[0]
    out = None
    for b in range(R):
        total = None
        for a in range(R):
            if table[a][b] > 0.0:
                term = table[a][b] * sums[a]
                total = term if total is None else total + term
        mid = total[1 : blocks - 1]
        if b == 0:
            out = mid
            continue
        lane = iota(mid.shape, 3)
        upper = jnp.where(lane < b, total[2:], mid)
        lower = jnp.where(lane >= LANES - b, total[: blocks - 2], mid)
        out = out + pltpu.roll(upper, LANES - b, 3) + pltpu.roll(lower, b, 3)
    return out


def kernel(
    gxn,
    gzn,
    fields,
    coef,
    plane_z,
    snap_index,
    fwd_hbm,
    design_hbm,
    sens_hbm,
    out,
    gradient,
    fwd,
    design,
    sens_in,
    E,
    H,
    C,
    EY,
    HY,
    exr,
    ezr,
    gxr,
    gzr,
    cxr,
    czr,
    gxs,
    gzs,
    AG,
    DF,
    L,
    SL,
    PT,
    RC,
    WV,
    step_send,
    step_recv,
    ag_send,
    ag_recv,
    rc_send,
    rc_recv,
    row_send,
    row_recv,
    load_sem,
):
    X, Z = coef.shape[0], coef.shape[1]
    NB = coef.shape[2]
    TB = NB // gzn
    WB = TB + 2
    gx, gz = lax.axis_index("gx"), lax.axis_index("gz")
    has_xm, has_xp = gx > 0, gx < gxn - 1
    has_zm, has_zp = gz > 0, gz < gzn - 1

    def load(index, src, dst):
        return pltpu.make_async_copy(src, dst, load_sem.at[index])

    half = X // 2
    loads = [
        load(0, fields.at[0:3, X - 1], E.at[:, X - 1, 0:Z]),
        load(1, fields.at[3:6, X - 1], H.at[:, X, 1 : Z + 1]),
        load(2, fields.at[0:3, 0 : X - 1, Z - 1], E.at[:, 0 : X - 1, Z - 1]),
        load(3, fields.at[3:6, 0 : X - 1, Z - 1], H.at[:, 1:X, Z]),
        load(4, fwd_hbm, fwd),
        load(5, design_hbm, design),
        load(6, sens_hbm, sens_in),
        load(7, fields.at[0:3, 0 : X - 1, 0 : Z - 1], E.at[:, 0 : X - 1, 0 : Z - 1]),
        load(8, fields.at[3:6, 0:half, 0 : Z - 1], H.at[:, 1 : half + 1, 1:Z]),
        load(9, coef.at[0:half], C.at[0:half]),
        load(10, fields.at[3:6, half : X - 1, 0 : Z - 1], H.at[:, half + 1 : X, 1:Z]),
        load(11, coef.at[half:X], C.at[half:X]),
    ]
    for copy in loads:
        copy.start()

    barrier = pltpu.get_barrier_semaphore()

    def greet(x, z):
        pl.semaphore_signal(barrier, inc=1, device_id={"gx": x, "gz": z}, device_id_type=MESH)

    for condition, x, z in (
        (has_xm, gx - 1, gz),
        (has_xp, gx + 1, gz),
        (has_xp & has_zm, gx + 1, gz - 1),
        (has_xm & has_zp, gx - 1, gz + 1),
    ):
        pl.when(condition)(functools.partial(greet, x, z))
    for d in range(1, gzn):
        greet(gx, lax.rem(gz + d, gzn))

    pads = jnp.zeros((2, 2 * PLANES, X, LANES), jnp.float32)
    AG[0:2, DESIGN:] = pads
    AG[NB + 2 :, DESIGN:] = pads
    PT[0] = jnp.zeros(PT.shape[1:], jnp.float32)
    PT[NB + 1] = jnp.zeros(PT.shape[1:], jnp.float32)
    DF[:, :, 0:R] = jnp.zeros((TB + 4, PLANES, R, LANES), jnp.float32)
    DF[:, :, R + X :] = jnp.zeros((TB + 4, PLANES, R, LANES), jnp.float32)

    E[:, X] = jnp.zeros((COMPS, Z + 1, SUBS, LANES), jnp.float32)
    E[:, 0:X, Z] = jnp.zeros((COMPS, X, SUBS, LANES), jnp.float32)
    H[:, 0] = jnp.zeros((COMPS, Z + 1, SUBS, LANES), jnp.float32)
    H[:, 1:, 0] = jnp.zeros((COMPS, X, SUBS, LANES), jnp.float32)

    met = (
        has_xm.astype(jnp.int32)
        + has_xp.astype(jnp.int32)
        + (has_xp & has_zm).astype(jnp.int32)
        + (has_xm & has_zp).astype(jnp.int32)
        + (gzn - 1)
    )
    pl.semaphore_wait(barrier, met)

    def remote(src, dst, send, recv, x, z):
        return pltpu.make_async_remote_copy(
            src_ref=src,
            dst_ref=dst,
            send_sem=send,
            recv_sem=recv,
            device_id={"gx": x, "gz": z},
            device_id_type=MESH,
        )

    def step_copies(s):
        electric = fields if s == 0 else E

        def make(k, src, dst, x, z):
            return remote(src, dst, step_send.at[s, k], step_recv.at[s, k], x, z)

        return dict(
            ex=(make(0, electric.at[1:3, 0, 0:Z], exr.at[s], gx - 1, gz), has_xm, has_xp),
            ez=(make(1, electric.at[0:2, 0:X, 0], ezr.at[s], gx, gz - 1), has_zm, has_zp),
            cx=(
                make(2, electric.at[0, X - 1, 0], cxr.at[s], gx + 1, gz - 1),
                has_xp & has_zm,
                has_xm & has_zp,
            ),
            cz=(
                make(3, electric.at[2, 0, Z - 1], czr.at[s], gx - 1, gz + 1),
                has_xm & has_zp,
                has_xp & has_zm,
            ),
            gx=(make(4, gxs.at[s], gxr.at[s], gx + 1, gz), has_xp, has_xm),
            gz=(make(5, gzs.at[s], gzr.at[s], gx, gz + 1), has_zp, has_zm),
        )

    def start(item):
        pl.when(item[1])(item[0].start)

    def finish_send(item):
        pl.when(item[1])(item[0].wait_send)

    def fill_sends(s):
        E[0, X - 1, Z] = jnp.zeros((SUBS, LANES), jnp.float32)
        E[2, X, Z - 1] = jnp.zeros((SUBS, LANES), jnp.float32)
        ex, ey, ez = (E[c, X - 1, 0:Z] for c in range(3))
        gxs[s, 0] = H[1, X, 1:] + magnetic_step * (E[0, X - 1, 1 : Z + 1] - ex + ez)
        gxs[s, 1] = H[2, X, 1:] - magnetic_step * (ey + ahead_y(ex) - ex)
        ex, ey, ez = (E[c, 0:X, Z - 1] for c in range(3))
        gzs[s, 0] = H[0, 1:, Z] + magnetic_step * (ahead_y(ez) - ez + ey)
        gzs[s, 1] = H[1, 1:, Z] - magnetic_step * (ex + E[2, 1 : X + 1, Z - 1] - ez)

    def receive(s, copies):
        @pl.when(has_xp)
        def _():
            copies["ex"][0].wait_recv()
            E[1:3, X, 0:Z] = exr[s]

        @pl.when(has_zp)
        def _():
            copies["ez"][0].wait_recv()
            E[0:2, 0:X, Z] = ezr[s]

        @pl.when(has_xm)
        def _():
            copies["gx"][0].wait_recv()
            H[1, 0, 1:] = gxr[s, 0] - magnetic_step * E[2, 0, 0:Z]
            H[2, 0, 1:] = gxr[s, 1] + magnetic_step * E[1, 0, 0:Z]

        @pl.when(has_zm)
        def _():
            copies["gz"][0].wait_recv()
            H[0, 1:, 0] = gzr[s, 0] - magnetic_step * E[1, 0:X, 0]
            H[1, 1:, 0] = gzr[s, 1] + magnetic_step * E[0, 0:X, 0]

        @pl.when(has_xm & has_zp)
        def _():
            copies["cx"][0].wait_recv()
            H[1, 0, Z] = H[1, 0, Z] + magnetic_step * cxr[s]

        @pl.when(has_xp & has_zm)
        def _():
            copies["cz"][0].wait_recv()
            H[1, X, 0] = H[1, X, 0] - magnetic_step * czr[s]

    def curl_h(e, next_x, next_z):
        (ex, ey, ez), (ey_x, ez_x), (ex_z, ey_z) = e, next_x, next_z
        return (
            magnetic_step * ((ahead_y(ez) - ez) - (ey_z - ey)),
            magnetic_step * ((ex_z - ex) - (ez_x - ez)),
            magnetic_step * ((ey_x - ey) - (ahead_y(ex) - ex)),
        )

    def new_e(e, h, before_x, before_z, factor):
        (hx, hy, hz), (hy_x, hz_x), (hx_z, hy_z) = h, before_x, before_z
        return (
            e[0] - factor * ((hz - behind_y(hz)) - (hy - hy_z)),
            e[1] - factor * ((hx - hx_z) - (hz - hz_x)),
            e[2] - factor * ((hy - hy_x) - (hx - behind_y(hx))),
        )

    CHUNKS = [(z, min(8, Z - z)) for z in range(0, Z, 8)]

    def shift_e(x):
        for z, n in CHUNKS:
            EY[0, z : z + n] = ahead_y(E[0, x, z : z + n])
            EY[1, z : z + n] = ahead_y(E[2, x, z : z + n])

    def shift_h(x):
        for z, n in CHUNKS:
            HY[0, z : z + n] = behind_y(H[0, x + 1, z + 1 : z + n + 1])
            HY[1, z : z + n] = behind_y(H[2, x + 1, z + 1 : z + n + 1])

    def layer_h(s, x):
        for z, n in CHUNKS:
            own, up = slice(z, z + n), slice(z + 1, z + n + 1)
            ex, ey, ez = (E[c, x, own] for c in range(COMPS))
            h = (
                H[0, x + 1, up] + magnetic_step * ((EY[1, own] - ez) - (E[1, x, up] - ey)),
                H[1, x + 1, up]
                + magnetic_step * ((E[0, x, up] - ex) - (E[2, x + 1, own] - ez)),
                H[2, x + 1, up] + magnetic_step * ((E[1, x + 1, own] - ey) - (EY[0, own] - ex)),
            )
            for c in range(COMPS):
                H[c, x + 1, up] = h[c]
                if s + 1 == STEPS:
                    out[COMPS + c, x, own] = h[c]

    def layer_e(s, x):
        for z, n in CHUNKS:
            own, up = slice(z, z + n), slice(z + 1, z + n + 1)
            hx, hy, hz = (H[c, x + 1, up] for c in range(COMPS))
            factor = C[x, own]
            e = (
                E[0, x, own] - factor * ((hz - HY[1, own]) - (hy - H[1, x + 1, own])),
                E[1, x, own] - factor * ((hx - H[0, x + 1, own]) - (hz - H[2, x, up])),
                E[2, x, own] - factor * ((hy - H[1, x, up]) - (hx - HY[0, own])),
            )
            for c in range(COMPS):
                if s + 1 == STEPS:
                    out[c, x, own] = e[c]
                else:
                    E[c, x, own] = e[c]

    def sweep(s, x_start, x_stop):
        if x_start == 0:
            shift_e(0)
            layer_h(s, 0)
            shift_e(1)
            shift_h(0)

        @pl.loop(max(x_start, 1), x_stop)
        def _(x):
            layer_h(s, x)
            layer_e(s, x - 1)
            shift_e(x + 1)
            shift_h(x)

        if x_stop == X:
            layer_e(s, X - 1)

    def layer_of(p):
        local = plane_z[p] - gz * Z
        inside = (local >= 0) & (local < Z)
        return jnp.clip(local, 0, Z - 1), jnp.where(inside, 1.0, 0.0).astype(jnp.float32)

    def products(step):
        @pl.loop(0, NB)
        def _(block):
            for p in range(PLANES):
                total = None
                for c in range(COMPS):
                    image = (step * PLANES + p) * COMPS + c
                    term = AG[block + 2, image] * L[step, p, c, :, block]
                    total = term if total is None else total + term
                if step:
                    total = PT[block + 1, p] + total
                PT[block + 1, p] = total

    def plane_e(layer):
        def h_at(z):
            e = tuple(E[c, 0:X, z] for c in range(COMPS))
            curl = curl_h(
                e, (E[1, 1 : X + 1, z], E[2, 1 : X + 1, z]), (E[0, 0:X, z + 1], E[1, 0:X, z + 1])
            )
            return e, tuple(H[c, 1 : X + 1, z + 1] + curl[c] for c in range(COMPS))

        e, h = h_at(layer)
        _, under = h_at(jnp.maximum(layer - 1, 0))
        lowest = layer == 0
        before_z = tuple(jnp.where(lowest, H[c, 1 : X + 1, 0], under[c]) for c in range(2))
        before_x = tuple(
            jnp.concatenate([H[c, 0:1, layer + 1], h[c][:-1]], axis=0) for c in (1, 2)
        )
        return new_e(e, h, before_x, before_z, C[0:X, layer])

    copies = step_copies(0)
    for name in ("ex", "ez", "cx", "cz"):
        start(copies[name])
    for copy in loads[:4]:
        copy.wait()
    fill_sends(0)
    start(copies["gx"])
    start(copies["gz"])
    for copy in loads[4:7]:
        copy.wait()
    snap = snap_index[0]
    for block in range(TB):
        lanes = slice(block * LANES, (block + 1) * LANES)
        place = 2 + gz * TB + block
        for step in range(STEPS):
            for p in range(PLANES):
                for c in range(COMPS):
                    AG[place, (step * PLANES + p) * COMPS + c] = fwd[snap + step, p, c, :, lanes]
        AG[place, DESIGN:SENS] = design[:, :, lanes]
        AG[place, SENS:] = sens_in[:, :, lanes]
    tile = pl.ds(2 + gz * TB, TB)
    gathers = [
        remote(AG.at[tile], AG.at[tile], ag_send.at[d], ag_recv.at[d], gx, lax.rem(gz + d, gzn))
        for d in range(1, gzn)
    ]
    for copy in gathers:
        copy.start()
    for copy in loads[7:10]:
        copy.wait()
    receive(0, copies)
    sweep(0, 0, half)
    for copy in loads[10:]:
        copy.wait()
    sweep(0, half, X)
    for item in copies.values():
        finish_send(item)

    copies = step_copies(1)
    for name in ("ex", "ez", "cx", "cz"):
        start(copies[name])
    fill_sends(1)
    start(copies["gx"])
    start(copies["gz"])
    for p in range(PLANES):
        layer, inside = layer_of(p)
        for c in range(COMPS):
            L[0, p, c] = E[c, 0:X, layer] * inside
    for d in range(1, gzn):
        source = pl.ds(2 + lax.rem(gz + gzn - d, gzn) * TB, TB)
        remote(
            AG.at[tile], AG.at[source], ag_send.at[d], ag_recv.at[d], gx, lax.rem(gz + d, gzn)
        ).wait_recv()
    around = pl.ds(gz * TB, TB + 4)
    rows = [
        (
            remote(
                AG.at[around, DESIGN:SENS, X - R : X],
                DF.at[:, :, 0:R],
                row_send.at[0],
                row_recv.at[0],
                gx + 1,
                gz,
            ),
            has_xp,
            has_xm,
        ),
        (
            remote(
                AG.at[around, DESIGN:SENS, 0:R],
                DF.at[:, :, R + X : X + 2 * R],
                row_send.at[1],
                row_recv.at[1],
                gx - 1,
                gz,
            ),
            has_xm,
            has_xp,
        ),
    ]
    for item in rows:
        start(item)
    products(0)

    DF[:, :, R : R + X] = AG[around, DESIGN:SENS]
    for item in rows:
        pl.when(item[2])(item[0].wait_recv)
    SL[...] = projection_slope(cone(DF, X))
    receive(1, copies)

    for p in range(PLANES):
        layer, inside = layer_of(p)
        for c, value in enumerate(plane_e(layer)):
            L[1, p, c] = value * inside
    products(1)
    partials = []
    for d in range(1, gzn):
        peer = lax.rem(gz + d, gzn)
        partials.append(
            remote(
                PT.at[pl.ds(peer * TB, WB)],
                RC.at[d],
                rc_send.at[d],
                rc_recv.at[d],
                gx,
                peer,
            )
        )
    for copy in partials:
        copy.start()
    sweep(1, 0, X)
    total = AG[pl.ds(gz * TB + 1, WB), SENS:] + PT[pl.ds(gz * TB, WB)]
    for d, copy in enumerate(partials, 1):
        copy.wait_recv()
        total = total + RC[d]
    WV[:, :, R : R + X] = total * SL[...]
    edges = [
        (
            remote(
                WV.at[:, :, X : X + R], WV.at[:, :, 0:R], row_send.at[2], row_recv.at[2], gx + 1, gz
            ),
            has_xp,
            has_xm,
        ),
        (
            remote(
                WV.at[:, :, R : 2 * R],
                WV.at[:, :, R + X : X + 2 * R],
                row_send.at[3],
                row_recv.at[3],
                gx - 1,
                gz,
            ),
            has_xm,
            has_xp,
        ),
    ]
    for item in edges:
        start(item)
    none = jnp.zeros((WB, PLANES, R, LANES), jnp.float32)

    @pl.when(gx == 0)
    def _():
        WV[:, :, 0:R] = none

    @pl.when(gx == gxn - 1)
    def _():
        WV[:, :, R + X :] = none

    for item in edges:
        pl.when(item[2])(item[0].wait_recv)
    result = cone(WV, X)
    for block in range(TB):
        gradient[:, :, block * LANES : (block + 1) * LANES] = result[block]

    for copy in gathers + partials:
        copy.wait_send()
    for item in rows + edges + list(copies.values()):
        finish_send(item)


def shards(adj_fields, coef_e, plane_z, snap_index, fwd_snaps, design, sens_in):
    gxn, gzn = lax.axis_size("gx"), lax.axis_size("gz")
    X, Z, NB = coef_e.shape[0], coef_e.shape[1], coef_e.shape[2]
    TB = NB // gzn
    WB = TB + 2
    cell = (SUBS, LANES)

    def vmem(*shape):
        return pltpu.VMEM(shape, jnp.float32)

    hbm = pl.BlockSpec(memory_space=pltpu.HBM)
    smem = pl.BlockSpec(memory_space=pltpu.SMEM)
    local = pl.BlockSpec(memory_space=pltpu.VMEM)
    dma = pltpu.SemaphoreType.DMA
    return pl.pallas_call(
        functools.partial(kernel, gxn, gzn),
        out_shape=(
            pltpu.VMEM(adj_fields.shape, jnp.float32),
            pltpu.VMEM(design.shape, jnp.float32),
        ),
        in_specs=[hbm, hbm, smem, smem, hbm, hbm, hbm],
        out_specs=(local, local),
        scratch_shapes=[
            vmem(*fwd_snaps.shape),
            vmem(*design.shape),
            vmem(*sens_in.shape),
            vmem(COMPS, X + 1, Z + 1, *cell),
            vmem(COMPS, X + 1, Z + 1, *cell),
            vmem(X, Z, *cell),
            vmem(2, Z, *cell),
            vmem(2, Z, *cell),
            vmem(STEPS, 2, Z, *cell),
            vmem(STEPS, 2, X, *cell),
            vmem(STEPS, 2, Z, *cell),
            vmem(STEPS, 2, X, *cell),
            vmem(STEPS, *cell),
            vmem(STEPS, *cell),
            vmem(STEPS, 2, Z, *cell),
            vmem(STEPS, 2, X, *cell),
            vmem(NB + 4, IMAGES, X, LANES),
            vmem(TB + 4, PLANES, X + 2 * R, LANES),
            vmem(STEPS, PLANES, COMPS, X, *cell),
            vmem(WB, PLANES, X, LANES),
            vmem(NB + 2, PLANES, X, LANES),
            vmem(gzn, WB, PLANES, X, LANES),
            vmem(WB, PLANES, X + 2 * R, LANES),
            dma((STEPS, 6)),
            dma((STEPS, 6)),
            dma((gzn,)),
            dma((gzn,)),
            dma((gzn,)),
            dma((gzn,)),
            dma((4,)),
            dma((4,)),
            dma((12,)),
        ],
        compiler_params=pltpu.CompilerParams(
            collective_id=0, has_side_effects=True, vmem_limit_bytes=51 * 2**20
        ),
    )(adj_fields, coef_e, plane_z, snap_index, fwd_snaps, design, sens_in)


def solution(mesh):
    in_specs = (
        P(None, "gx", "gz", None, None),
        P("gx", "gz", None, None),
        P(),
        P(),
        P(None, None, None, "gx", "gz"),
        P(None, "gx", "gz"),
        P(None, "gx", "gz"),
    )
    out_specs = (P(None, "gx", "gz", None, None), P(None, "gx", "gz"))
    return jax.shard_map(shards, mesh=mesh, in_specs=in_specs, out_specs=out_specs, check_vma=False)
```

```python
import functools
import math

import jax
import jax.numpy as jnp
from jax import lax
from jax.experimental import pallas as pl
from jax.experimental.pallas import tpu as pltpu
from jax.sharding import PartitionSpec as P

R = 8
STEPS = 2
PLANES = 2
COMPS = 3
IMAGES = STEPS * PLANES * COMPS + 2 * PLANES
DESIGN = STEPS * PLANES * COMPS
SENS = DESIGN + PLANES
LANES = 128
SUBS = 8

magnetic_step = 0.5
sharpness = 8.0
threshold = 0.5

MESH = pl.DeviceIdType.MESH


def cone_table(radius):
    raw = [
        [max(0.0, radius - math.sqrt(a * a + b * b)) for b in range(radius + 1)]
        for a in range(radius + 1)
    ]
    total = sum(
        raw[abs(a)][abs(b)]
        for a in range(-radius, radius + 1)
        for b in range(-radius, radius + 1)
    )
    return [[entry / total for entry in line] for line in raw]


def projection_slope(filtered):
    scale_down = math.tanh(sharpness * threshold) + math.tanh(sharpness * (1.0 - threshold))
    return sharpness * (1.0 - jnp.tanh(sharpness * (filtered - threshold)) ** 2) / scale_down


def iota(shape, dim):
    return lax.broadcasted_iota(jnp.int32, shape, dim)


def ahead_y(v):
    n = v.ndim
    turned = pltpu.roll(v, LANES - 1, n - 1)
    carried = pltpu.roll(turned, SUBS - 1, n - 2)
    carried = jnp.where(iota(v.shape, n - 2) == SUBS - 1, 0.0, carried)
    return jnp.where(iota(v.shape, n - 1) == LANES - 1, carried, turned)


def behind_y(v):
    n = v.ndim
    turned = pltpu.roll(v, 1, n - 1)
    carried = pltpu.roll(turned, 1, n - 2)
    carried = jnp.where(iota(v.shape, n - 2) == 0, 0.0, carried)
    return jnp.where(iota(v.shape, n - 1) == 0, carried, turned)


def ahead_pair(a, b):
    n = a.ndim
    sub, lane = iota(a.shape, n - 2), iota(a.shape, n - 1)
    turned = pltpu.roll(b, LANES - 1, n - 1)
    carried = pltpu.roll(jnp.where(lane == 0, a, turned), SUBS - 1, n - 2)
    carried = jnp.where(sub == SUBS - 1, 0.0, carried)
    first = pltpu.roll(jnp.where(lane == 0, carried, a), LANES - 1, n - 1)
    return first, jnp.where(lane == LANES - 1, carried, turned)


def behind_pair(a, b):
    n = a.ndim
    sub, lane = iota(a.shape, n - 2), iota(a.shape, n - 1)
    turned = pltpu.roll(b, 1, n - 1)
    carried = pltpu.roll(jnp.where(lane == LANES - 1, a, turned), 1, n - 2)
    carried = jnp.where(sub == 0, 0.0, carried)
    first = pltpu.roll(jnp.where(lane == LANES - 1, carried, a), 1, n - 1)
    return first, jnp.where(lane == 0, carried, turned)


def cone(ref, p, rows):
    table = cone_table(R)
    sums = [ref[:, p, R : R + rows]]
    for a in range(1, R):
        sums.append(ref[:, p, R - a : R - a + rows] + ref[:, p, R + a : R + a + rows])
    blocks = ref.shape[0]
    out = None
    for b in range(R):
        total = None
        for a in range(R):
            if table[a][b] > 0.0:
                term = table[a][b] * sums[a]
                total = term if total is None else total + term
        mid = total[1 : blocks - 1]
        if b == 0:
            out = mid
            continue
        lane = iota(mid.shape, 2)
        upper = jnp.where(lane < b, total[2:], mid)
        lower = jnp.where(lane >= LANES - b, total[: blocks - 2], mid)
        out = out + pltpu.roll(upper, LANES - b, 2) + pltpu.roll(lower, b, 2)
    return out


def kernel(
    gxn,
    gzn,
    fields,
    coef,
    plane_z,
    snap_index,
    fwd_hbm,
    design_hbm,
    sens_hbm,
    out,
    gradient,
    fwd,
    design,
    sens_in,
    E,
    H,
    C,
    EY,
    HY,
    exr,
    ezr,
    gxr,
    gzr,
    cxr,
    czr,
    gxs,
    gzs,
    AG,
    DF,
    L,
    SL,
    PT,
    RC,
    WV,
    step_send,
    step_recv,
    ag_send,
    ag_recv,
    rc_send,
    rc_recv,
    row_send,
    row_recv,
    load_sem,
):
    X, Z = coef.shape[0], coef.shape[1]
    NB = coef.shape[2]
    TB = NB // gzn
    WB = TB + 2
    gx, gz = lax.axis_index("gx"), lax.axis_index("gz")
    has_xm, has_xp = gx > 0, gx < gxn - 1
    has_zm, has_zp = gz > 0, gz < gzn - 1

    def load(index, src, dst):
        return pltpu.make_async_copy(src, dst, load_sem.at[index])

    half = X // 2
    loads = [
        load(0, fields.at[0:3, X - 1], E.at[:, X - 1, 0:Z]),
        load(1, fields.at[3:6, X - 1], H.at[:, X, 1 : Z + 1]),
        load(2, fields.at[0:3, 0 : X - 1, Z - 1], E.at[:, 0 : X - 1, Z - 1]),
        load(3, fields.at[3:6, 0 : X - 1, Z - 1], H.at[:, 1:X, Z]),
        load(4, fwd_hbm, fwd),
        load(5, design_hbm, design),
        load(6, sens_hbm, sens_in),
        load(7, fields.at[0:3, 0 : X - 1, 0 : Z - 1], E.at[:, 0 : X - 1, 0 : Z - 1]),
        load(8, fields.at[3:6, 0:half, 0 : Z - 1], H.at[:, 1 : half + 1, 1:Z]),
        load(9, coef.at[0:half], C.at[0:half]),
        load(10, fields.at[3:6, half : X - 1, 0 : Z - 1], H.at[:, half + 1 : X, 1:Z]),
        load(11, coef.at[half:X], C.at[half:X]),
    ]
    for copy in loads:
        copy.start()

    barrier = pltpu.get_barrier_semaphore()

    def greet(x, z):
        pl.semaphore_signal(barrier, inc=1, device_id={"gx": x, "gz": z}, device_id_type=MESH)

    for condition, x, z in (
        (has_xm, gx - 1, gz),
        (has_xp, gx + 1, gz),
        (has_xp & has_zm, gx + 1, gz - 1),
        (has_xm & has_zp, gx - 1, gz + 1),
    ):
        pl.when(condition)(functools.partial(greet, x, z))
    for d in range(1, gzn):
        greet(gx, lax.rem(gz + d, gzn))

    pads = jnp.zeros((2, 2 * PLANES, X, LANES), jnp.float32)
    AG[0:2, DESIGN:] = pads
    AG[NB + 2 :, DESIGN:] = pads
    PT[0] = jnp.zeros(PT.shape[1:], jnp.float32)
    PT[NB + 1] = jnp.zeros(PT.shape[1:], jnp.float32)
    DF[:, :, 0:R] = jnp.zeros((TB + 4, PLANES, R, LANES), jnp.float32)
    DF[:, :, R + X :] = jnp.zeros((TB + 4, PLANES, R, LANES), jnp.float32)

    E[:, X] = jnp.zeros((COMPS, Z + 1, SUBS, LANES), jnp.float32)
    E[:, 0:X, Z] = jnp.zeros((COMPS, X, SUBS, LANES), jnp.float32)
    H[:, 0] = jnp.zeros((COMPS, Z + 1, SUBS, LANES), jnp.float32)
    H[:, 1:, 0] = jnp.zeros((COMPS, X, SUBS, LANES), jnp.float32)

    met = (
        has_xm.astype(jnp.int32)
        + has_xp.astype(jnp.int32)
        + (has_xp & has_zm).astype(jnp.int32)
        + (has_xm & has_zp).astype(jnp.int32)
        + (gzn - 1)
    )
    pl.semaphore_wait(barrier, met)

    def remote(src, dst, send, recv, x, z):
        return pltpu.make_async_remote_copy(
            src_ref=src,
            dst_ref=dst,
            send_sem=send,
            recv_sem=recv,
            device_id={"gx": x, "gz": z},
            device_id_type=MESH,
        )

    def step_copies(s):
        electric = fields if s == 0 else E

        def make(k, src, dst, x, z):
            return remote(src, dst, step_send.at[s, k], step_recv.at[s, k], x, z)

        return dict(
            ex=(make(0, electric.at[1:3, 0, 0:Z], exr.at[s], gx - 1, gz), has_xm, has_xp),
            ez=(make(1, electric.at[0:2, 0:X, 0], ezr.at[s], gx, gz - 1), has_zm, has_zp),
            cx=(
                make(2, electric.at[0, X - 1, 0], cxr.at[s], gx + 1, gz - 1),
                has_xp & has_zm,
                has_xm & has_zp,
            ),
            cz=(
                make(3, electric.at[2, 0, Z - 1], czr.at[s], gx - 1, gz + 1),
                has_xm & has_zp,
                has_xp & has_zm,
            ),
            gx=(make(4, gxs.at[s], gxr.at[s], gx + 1, gz), has_xp, has_xm),
            gz=(make(5, gzs.at[s], gzr.at[s], gx, gz + 1), has_zp, has_zm),
        )

    def start(item):
        pl.when(item[1])(item[0].start)

    def finish_send(item):
        pl.when(item[1])(item[0].wait_send)

    def fill_sends(s):
        E[0, X - 1, Z] = jnp.zeros((SUBS, LANES), jnp.float32)
        E[2, X, Z - 1] = jnp.zeros((SUBS, LANES), jnp.float32)
        ex, ey, ez = (E[c, X - 1, 0:Z] for c in range(3))
        gxs[s, 0] = H[1, X, 1:] + magnetic_step * (E[0, X - 1, 1 : Z + 1] - ex + ez)
        gxs[s, 1] = H[2, X, 1:] - magnetic_step * (ey + ahead_y(ex) - ex)
        ex, ey, ez = (E[c, 0:X, Z - 1] for c in range(3))
        gzs[s, 0] = H[0, 1:, Z] + magnetic_step * (ahead_y(ez) - ez + ey)
        gzs[s, 1] = H[1, 1:, Z] - magnetic_step * (ex + E[2, 1 : X + 1, Z - 1] - ez)

    def receive(s, copies):
        @pl.when(has_xp)
        def _():
            copies["ex"][0].wait_recv()
            E[1:3, X, 0:Z] = exr[s]

        @pl.when(has_zp)
        def _():
            copies["ez"][0].wait_recv()
            E[0:2, 0:X, Z] = ezr[s]

        @pl.when(has_xm)
        def _():
            copies["gx"][0].wait_recv()
            H[1, 0, 1:] = gxr[s, 0] - magnetic_step * E[2, 0, 0:Z]
            H[2, 0, 1:] = gxr[s, 1] + magnetic_step * E[1, 0, 0:Z]

        @pl.when(has_zm)
        def _():
            copies["gz"][0].wait_recv()
            H[0, 1:, 0] = gzr[s, 0] - magnetic_step * E[1, 0:X, 0]
            H[1, 1:, 0] = gzr[s, 1] + magnetic_step * E[0, 0:X, 0]

        @pl.when(has_xm & has_zp)
        def _():
            copies["cx"][0].wait_recv()
            H[1, 0, Z] = H[1, 0, Z] + magnetic_step * cxr[s]

        @pl.when(has_xp & has_zm)
        def _():
            copies["cz"][0].wait_recv()
            H[1, X, 0] = H[1, X, 0] - magnetic_step * czr[s]

    def curl_h(e, next_x, next_z):
        (ex, ey, ez), (ey_x, ez_x), (ex_z, ey_z) = e, next_x, next_z
        return (
            magnetic_step * ((ahead_y(ez) - ez) - (ey_z - ey)),
            magnetic_step * ((ex_z - ex) - (ez_x - ez)),
            magnetic_step * ((ey_x - ey) - (ahead_y(ex) - ex)),
        )

    def new_e(e, h, before_x, before_z, factor):
        (hx, hy, hz), (hy_x, hz_x), (hx_z, hy_z) = h, before_x, before_z
        return (
            e[0] - factor * ((hz - behind_y(hz)) - (hy - hy_z)),
            e[1] - factor * ((hx - hx_z) - (hz - hz_x)),
            e[2] - factor * ((hy - hy_x) - (hx - behind_y(hx))),
        )

    CHUNKS = [(z, min(8, Z - z)) for z in range(0, Z, 8)]

    def shift_e(x):
        for z, n in CHUNKS:
            own = slice(z, z + n)
            EY[0, own], EY[1, own] = ahead_pair(E[0, x, own], E[2, x, own])

    def shift_h(x):
        for z, n in CHUNKS:
            own, up = slice(z, z + n), slice(z + 1, z + n + 1)
            HY[0, own], HY[1, own] = behind_pair(H[0, x + 1, up], H[2, x + 1, up])

    def layer_h(s, x):
        for z, n in CHUNKS:
            own, up = slice(z, z + n), slice(z + 1, z + n + 1)
            ex, ey, ez = (E[c, x, own] for c in range(COMPS))
            h = (
                H[0, x + 1, up] + magnetic_step * ((EY[1, own] - ez) - (E[1, x, up] - ey)),
                H[1, x + 1, up]
                + magnetic_step * ((E[0, x, up] - ex) - (E[2, x + 1, own] - ez)),
                H[2, x + 1, up] + magnetic_step * ((E[1, x + 1, own] - ey) - (EY[0, own] - ex)),
            )
            for c in range(COMPS):
                H[c, x + 1, up] = h[c]
                if s + 1 == STEPS:
                    out[COMPS + c, x, own] = h[c]

    def layer_e(s, x):
        for z, n in CHUNKS:
            own, up = slice(z, z + n), slice(z + 1, z + n + 1)
            hx, hy, hz = (H[c, x + 1, up] for c in range(COMPS))
            factor = C[x, own]
            e = (
                E[0, x, own] - factor * ((hz - HY[1, own]) - (hy - H[1, x + 1, own])),
                E[1, x, own] - factor * ((hx - H[0, x + 1, own]) - (hz - H[2, x, up])),
                E[2, x, own] - factor * ((hy - H[1, x, up]) - (hx - HY[0, own])),
            )
            for c in range(COMPS):
                if s + 1 == STEPS:
                    out[c, x, own] = e[c]
                else:
                    E[c, x, own] = e[c]

    def sweep(s, x_start, x_stop):
        if x_start == 0:
            shift_e(0)
            layer_h(s, 0)
            shift_e(1)
            shift_h(0)

        @pl.loop(max(x_start, 1), x_stop)
        def _(x):
            layer_h(s, x)
            layer_e(s, x - 1)
            shift_e(x + 1)
            shift_h(x)

        if x_stop == X:
            layer_e(s, X - 1)

    def layer_of(p):
        local = plane_z[p] - gz * Z
        inside = (local >= 0) & (local < Z)
        return jnp.clip(local, 0, Z - 1), jnp.where(inside, 1.0, 0.0).astype(jnp.float32)

    def products(step):
        @pl.loop(0, NB)
        def _(block):
            for p in range(PLANES):
                total = None
                for c in range(COMPS):
                    image = (step * PLANES + p) * COMPS + c
                    term = AG[block + 2, image] * L[step, p, c, :, block]
                    total = term if total is None else total + term
                if step:
                    total = PT[block + 1, p] + total
                PT[block + 1, p] = total

    def plane_e(layer):
        def h_at(z):
            e = tuple(E[c, 0:X, z] for c in range(COMPS))
            curl = curl_h(
                e, (E[1, 1 : X + 1, z], E[2, 1 : X + 1, z]), (E[0, 0:X, z + 1], E[1, 0:X, z + 1])
            )
            return e, tuple(H[c, 1 : X + 1, z + 1] + curl[c] for c in range(COMPS))

        e, h = h_at(layer)
        _, under = h_at(jnp.maximum(layer - 1, 0))
        lowest = layer == 0
        before_z = tuple(jnp.where(lowest, H[c, 1 : X + 1, 0], under[c]) for c in range(2))
        before_x = tuple(
            jnp.concatenate([H[c, 0:1, layer + 1], h[c][:-1]], axis=0) for c in (1, 2)
        )
        return new_e(e, h, before_x, before_z, C[0:X, layer])

    copies = step_copies(0)
    for name in ("ex", "ez", "cx", "cz"):
        start(copies[name])
    for copy in loads[:4]:
        copy.wait()
    fill_sends(0)
    start(copies["gx"])
    start(copies["gz"])
    for copy in loads[4:7]:
        copy.wait()
    snap = snap_index[0]
    for block in range(TB):
        lanes = slice(block * LANES, (block + 1) * LANES)
        place = 2 + gz * TB + block
        for step in range(STEPS):
            for p in range(PLANES):
                for c in range(COMPS):
                    AG[place, (step * PLANES + p) * COMPS + c] = fwd[snap + step, p, c, :, lanes]
        AG[place, DESIGN:SENS] = design[:, :, lanes]
        AG[place, SENS:] = sens_in[:, :, lanes]
    tile = pl.ds(2 + gz * TB, TB)
    gathers = [
        remote(AG.at[tile], AG.at[tile], ag_send.at[d], ag_recv.at[d], gx, lax.rem(gz + d, gzn))
        for d in range(1, gzn)
    ]
    for copy in gathers:
        copy.start()
    for copy in loads[7:10]:
        copy.wait()
    receive(0, copies)
    sweep(0, 0, half)
    for copy in loads[10:]:
        copy.wait()
    sweep(0, half, X)
    for item in copies.values():
        finish_send(item)

    copies = step_copies(1)
    for name in ("ex", "ez", "cx", "cz"):
        start(copies[name])
    fill_sends(1)
    start(copies["gx"])
    start(copies["gz"])
    for p in range(PLANES):
        layer, inside = layer_of(p)
        for c in range(COMPS):
            L[0, p, c] = E[c, 0:X, layer] * inside
    for d in range(1, gzn):
        source = pl.ds(2 + lax.rem(gz + gzn - d, gzn) * TB, TB)
        remote(
            AG.at[tile], AG.at[source], ag_send.at[d], ag_recv.at[d], gx, lax.rem(gz + d, gzn)
        ).wait_recv()
    around = pl.ds(gz * TB, TB + 4)
    rows = [
        (
            remote(
                AG.at[around, DESIGN:SENS, X - R : X],
                DF.at[:, :, 0:R],
                row_send.at[0],
                row_recv.at[0],
                gx + 1,
                gz,
            ),
            has_xp,
            has_xm,
        ),
        (
            remote(
                AG.at[around, DESIGN:SENS, 0:R],
                DF.at[:, :, R + X : X + 2 * R],
                row_send.at[1],
                row_recv.at[1],
                gx - 1,
                gz,
            ),
            has_xm,
            has_xp,
        ),
    ]
    for item in rows:
        start(item)
    products(0)

    DF[:, :, R : R + X] = AG[around, DESIGN:SENS]
    for item in rows:
        pl.when(item[2])(item[0].wait_recv)

    @pl.loop(0, PLANES)
    def _(p):
        SL[:, p] = projection_slope(cone(DF, p, X))

    receive(1, copies)

    for p in range(PLANES):
        layer, inside = layer_of(p)
        for c, value in enumerate(plane_e(layer)):
            L[1, p, c] = value * inside
    products(1)
    partials = []
    for d in range(1, gzn):
        peer = lax.rem(gz + d, gzn)
        partials.append(
            remote(
                PT.at[pl.ds(peer * TB, WB)],
                RC.at[d],
                rc_send.at[d],
                rc_recv.at[d],
                gx,
                peer,
            )
        )
    for copy in partials:
        copy.start()
    sweep(1, 0, X)
    total = AG[pl.ds(gz * TB + 1, WB), SENS:] + PT[pl.ds(gz * TB, WB)]
    for d, copy in enumerate(partials, 1):
        copy.wait_recv()
        total = total + RC[d]
    WV[:, :, R : R + X] = total * SL[...]
    edges = [
        (
            remote(
                WV.at[:, :, X : X + R], WV.at[:, :, 0:R], row_send.at[2], row_recv.at[2], gx + 1, gz
            ),
            has_xp,
            has_xm,
        ),
        (
            remote(
                WV.at[:, :, R : 2 * R],
                WV.at[:, :, R + X : X + 2 * R],
                row_send.at[3],
                row_recv.at[3],
                gx - 1,
                gz,
            ),
            has_xm,
            has_xp,
        ),
    ]
    for item in edges:
        start(item)
    none = jnp.zeros((WB, PLANES, R, LANES), jnp.float32)

    @pl.when(gx == 0)
    def _():
        WV[:, :, 0:R] = none

    @pl.when(gx == gxn - 1)
    def _():
        WV[:, :, R + X :] = none

    for item in edges:
        pl.when(item[2])(item[0].wait_recv)

    @pl.loop(0, PLANES)
    def _(p):
        result = cone(WV, p, X)
        for block in range(TB):
            gradient[p, :, block * LANES : (block + 1) * LANES] = result[block]


    for copy in gathers + partials:
        copy.wait_send()
    for item in rows + edges + list(copies.values()):
        finish_send(item)


def shards(adj_fields, coef_e, plane_z, snap_index, fwd_snaps, design, sens_in):
    gxn, gzn = lax.axis_size("gx"), lax.axis_size("gz")
    X, Z, NB = coef_e.shape[0], coef_e.shape[1], coef_e.shape[2]
    TB = NB // gzn
    WB = TB + 2
    cell = (SUBS, LANES)

    def vmem(*shape):
        return pltpu.VMEM(shape, jnp.float32)

    hbm = pl.BlockSpec(memory_space=pltpu.HBM)
    smem = pl.BlockSpec(memory_space=pltpu.SMEM)
    local = pl.BlockSpec(memory_space=pltpu.VMEM)
    dma = pltpu.SemaphoreType.DMA
    return pl.pallas_call(
        functools.partial(kernel, gxn, gzn),
        out_shape=(
            pltpu.VMEM(adj_fields.shape, jnp.float32),
            pltpu.VMEM(design.shape, jnp.float32),
        ),
        in_specs=[hbm, hbm, smem, smem, hbm, hbm, hbm],
        out_specs=(local, local),
        scratch_shapes=[
            vmem(*fwd_snaps.shape),
            vmem(*design.shape),
            vmem(*sens_in.shape),
            vmem(COMPS, X + 1, Z + 1, *cell),
            vmem(COMPS, X + 1, Z + 1, *cell),
            vmem(X, Z, *cell),
            vmem(2, Z, *cell),
            vmem(2, Z, *cell),
            vmem(STEPS, 2, Z, *cell),
            vmem(STEPS, 2, X, *cell),
            vmem(STEPS, 2, Z, *cell),
            vmem(STEPS, 2, X, *cell),
            vmem(STEPS, *cell),
            vmem(STEPS, *cell),
            vmem(STEPS, 2, Z, *cell),
            vmem(STEPS, 2, X, *cell),
            vmem(NB + 4, IMAGES, X, LANES),
            vmem(TB + 4, PLANES, X + 2 * R, LANES),
            vmem(STEPS, PLANES, COMPS, X, *cell),
            vmem(WB, PLANES, X, LANES),
            vmem(NB + 2, PLANES, X, LANES),
            vmem(gzn, WB, PLANES, X, LANES),
            vmem(WB, PLANES, X + 2 * R, LANES),
            dma((STEPS, 6)),
            dma((STEPS, 6)),
            dma((gzn,)),
            dma((gzn,)),
            dma((gzn,)),
            dma((gzn,)),
            dma((4,)),
            dma((4,)),
            dma((12,)),
        ],
        compiler_params=pltpu.CompilerParams(
            collective_id=0, has_side_effects=True, vmem_limit_bytes=51 * 2**20
        ),
    )(adj_fields, coef_e, plane_z, snap_index, fwd_snaps, design, sens_in)


def solution(mesh):
    in_specs = (
        P(None, "gx", "gz", None, None),
        P("gx", "gz", None, None),
        P(),
        P(),
        P(None, None, None, "gx", "gz"),
        P(None, "gx", "gz"),
        P(None, "gx", "gz"),
    )
    out_specs = (P(None, "gx", "gz", None, None), P(None, "gx", "gz"))
    return jax.shard_map(shards, mesh=mesh, in_specs=in_specs, out_specs=out_specs, check_vma=False)
```
